32 devices in a mesh: region: 4 (over x, core), member: 8 (over z, y).
Axes of the slice: x: 2, y: 2, z: 4, core: 2. Of those that a mesh axis runs over, the one named last changes fastest.
Arguments:
- predicted_states: float32 [16, 100, 128, 128], P('member', None, 'region'), may hold values from -20 to 20, as said below
- observed_analysis: float32 [100, 128, 128], P(None, 'region'), may hold values from -20 to 20
- tile_location_sequence: int32 [4, 4096], P('region'), may hold values from 0 to 4095, each once within a row
Outputs:
- gradient: float32 [16, 100, 128, 128], P('member', None, 'region')
The draws below stay inside these ranges and needn't reach their ends.
Inputs may be any that keep to these rules, and one draw needn't show every extreme that they name: Each row of tile_location_sequence is a permutation of the cells of one region. `predicted_states`: members share a common field per variable and cell, with variable and cell scales.
All inputs are finite; a program needn't handle non-finite values.
Results may differ from the reference program's by a relative error of at most 0.0003.
Values sent between devices are 32-bit elements; how exact they have to be, the bound alone decides.
No kernel may reach another device: no remote copies, remote signals or barrier semaphores. Data moves between devices by JAX's collectives and lax.ppermute only.
A program may use at most 128 MiB of HBM per device.

```python
import jax
import jax.numpy as jnp
from jax import lax

V = 100
ROWS_DEV = 32
LON = 128
HALF = 32
PATCH = 128
MEMBERS = 16
REGIONS = 4
ROWS = 128
N_REGION = 4


def shared_parts(key):
    base = jax.random.fold_in(key, 101)
    first_key, second_key, third_key = jax.random.split(base, 3)
    common = jax.random.normal(first_key, (V, ROWS, LON), jnp.float32)
    var_scale = jnp.exp(jax.random.uniform(second_key, (V, 1, 1), jnp.float32, -1.15, 1.15))
    cell_scale = jnp.exp(jax.random.uniform(third_key, (1, ROWS, LON), jnp.float32, -0.7, 0.7))
    return (common, var_scale * cell_scale)


def draw_predicted_states(key, part):
    common, scales = shared_parts(key)
    noise = jax.random.normal(jax.random.fold_in(key, 202), (MEMBERS, V, ROWS, LON), jnp.float32)
    return jnp.clip(scales[None] * (common[None] + 0.6 * noise), -20.0, 20.0)


def draw_observed_analysis(key, part):
    common, scales = shared_parts(key)
    noise = jax.random.normal(jax.random.fold_in(key, 303), (V, ROWS, LON), jnp.float32)
    return jnp.clip(scales * (common + 0.6 * noise), -20.0, 20.0)


def setup_inputs(seed: int = 0) -> dict:
    arg_keys = jax.random.split(jax.random.key(seed), 4)
    return {
        "predicted_states": draw_predicted_states(jax.random.fold_in(arg_keys[3], 71), 0),
        "observed_analysis": draw_observed_analysis(jax.random.fold_in(arg_keys[3], 71), 0),
        "tile_location_sequence": jax.vmap(lambda own: jax.random.permutation(own, ROWS_DEV * LON))(jax.random.split(arg_keys[2], REGIONS)).reshape((REGIONS, ROWS_DEV * LON)).astype(jnp.int32),
    }


def kernel_value(offset, half):
    sigma = half / 2.0
    steps = jnp.arange(-half, half + 1).astype(jnp.float32)
    norm_sum = jnp.sum(jnp.exp(-(steps * steps) / (2.0 * sigma * sigma)))
    bell = jnp.exp(-(offset * offset) / (2.0 * sigma * sigma)) / norm_sum
    value = 0.5 * (offset == 0.0).astype(jnp.float32) + 0.5 * bell
    return jnp.where(jnp.abs(offset) <= half, value, jnp.zeros_like(value))

def lon_matrix():
    first = jnp.arange(LON)[:, None]
    second = jnp.arange(LON)[None, :]
    offset = second - first
    return kernel_value(offset.astype(jnp.float32), HALF)

def smooth_surface(values):
    along_lon = jnp.einsum('mrl,lk->mrk', values, lon_matrix(), precision=lax.Precision.HIGHEST)
    padded = jnp.pad(along_lon, ((0, 0), (HALF, HALF), (0, 0)))
    result = jnp.zeros_like(along_lon)
    for offset in range(-HALF, HALF + 1):
        weight = kernel_value(jnp.float32(offset), HALF)
        result = result + weight * padded[:, HALF + offset:HALF + offset + ROWS, :]
    return result

def reference(predicted_states, observed_analysis, tile_location_sequence):
    mesh_locations = ROWS_DEV * LON
    blocks = mesh_locations // PATCH
    region_index = jnp.arange(N_REGION).astype(jnp.int32)[:, None]

    def lone_quantity(pair):
        members_field, truth = pair
        softened_surface = smooth_surface(members_field)
        by_region = softened_surface.reshape(MEMBERS, N_REGION, mesh_locations)
        picked = by_region[:, region_index, tile_location_sequence].reshape(MEMBERS, N_REGION * blocks, PATCH)
        truth_picked = truth.reshape(N_REGION, mesh_locations)[region_index, tile_location_sequence].reshape(N_REGION * blocks, PATCH)
        diff = picked - truth_picked[None]
        toward = diff / jnp.sqrt(lax.optimization_barrier(jnp.sum(diff * diff, axis=-1, keepdims=True)) + 1e-06)
        inner_products = jnp.einsum('mkp,nkp->kmn', picked, picked, precision=lax.Precision.HIGHEST)
        squares = jnp.einsum('mkp,mkp->km', picked, picked, precision=lax.Precision.HIGHEST)
        dist_sq = jnp.maximum(squares[:, :, None] + squares[:, None, :] - 2.0 * inner_products, 0.0)
        self_pair = jnp.arange(MEMBERS)[:, None] == jnp.arange(MEMBERS)[None, :]
        pair_weights = jnp.where(self_pair[None], jnp.zeros_like(dist_sq), 1.0 / jnp.sqrt(dist_sq + 1e-06))
        pulled = lax.optimization_barrier(jnp.sum(pair_weights, axis=-1)).T
        apart = pulled[:, :, None] * picked - jnp.einsum('kmn,nkp->mkp', pair_weights, picked, precision=lax.Precision.HIGHEST)
        apart = apart / MEMBERS
        patch_grad = jnp.sqrt(jnp.float32(PATCH)) * (toward - apart)
        located_points = jnp.zeros((MEMBERS, N_REGION, mesh_locations), jnp.float32)
        located_points = located_points.at[:, region_index, tile_location_sequence].set(patch_grad.reshape(MEMBERS, N_REGION, mesh_locations))
        return smooth_surface(located_points.reshape(MEMBERS, ROWS, LON))
    layered_surfaces = lax.map(lone_quantity, (jnp.transpose(predicted_states, (1, 0, 2, 3)), observed_analysis))
    return jnp.transpose(layered_surfaces, (1, 0, 2, 3))
```

```python
import functools

import jax
import jax.numpy as jnp
import numpy as np
from jax import lax
from jax.experimental import pallas as pl
from jax.experimental.pallas import tpu as pltpu
from jax.sharding import PartitionSpec as P

HALF = 32
PATCH = 128
EPS = 1e-06
STEP = 4
VMEM = 56 * 1024 * 1024
F32 = jnp.float32
BF16 = jnp.bfloat16


def bell(out_cells, in_cells):
    sigma = HALF / 2.0
    steps = np.arange(-HALF, HALF + 1)
    norm = np.sum(np.exp(-(steps**2) / (2.0 * sigma**2)))
    offset = np.asarray(in_cells)[None, :] - np.asarray(out_cells)[:, None]
    value = 0.5 * np.exp(-(offset**2) / (2.0 * sigma**2)) / norm
    value = jnp.asarray(np.where(np.abs(offset) <= HALF, value, 0.0), F32)
    return halves(value)


def halves(x):
    head = x.astype(BF16)
    return head, (x - head.astype(F32)).astype(BF16)


def lon_weights(lon):
    head, tail = bell(range(lon), range(lon))
    return jnp.concatenate([head, head, tail], axis=0)


def lat_weights(rows, pad):
    head, tail = bell(range(rows), range(-pad, rows + pad))
    return jnp.concatenate([head, head, tail], axis=1)


def along_lon(x, weights):
    head, tail = halves(x)
    return 0.5 * x + jnp.dot(
        jnp.concatenate([head, tail, head], axis=1), weights, preferred_element_type=F32
    )


def along_lat(x, weights, own):
    head, tail = halves(x)
    return 0.5 * own + jnp.dot(
        weights, jnp.concatenate([head, tail, head], axis=0), preferred_element_type=F32
    )


def patch_sums(squares, hot):
    head, tail = halves(squares)
    return lax.dot_general(
        jnp.concatenate([head, tail], axis=0),
        hot,
        (((1,), (1,)), ((), ())),
        preferred_element_type=F32,
    )


def on_cells(weights, hot):
    return jnp.dot(weights, jnp.concatenate([hot, hot], axis=0), preferred_element_type=F32)


def head_and_tail(weights):
    return jnp.concatenate(halves(weights), axis=1)


def field_kernel(
    regions, me_ref, field_ref, truth_ref, map_ref, lon_ref, lat_ref, out_ref, cells, hots
):
    sources, _, held, rows, lon = field_ref.shape
    devices = sources // regions
    members = devices * held
    steps = rows // STEP
    patches = hots.shape[1]
    shifts = members // 2
    scale = float(np.sqrt(PATCH))

    @pl.when(pl.program_id(0) == 0)
    def _():
        patch = lax.broadcasted_iota(jnp.int32, (patches, lon), 0).astype(F32)

        def build(block, carry):
            for j in range(STEP):
                own = map_ref[pl.ds(block * STEP + j, 1), :]
                hots[block, :, j * lon : (j + 1) * lon] = (patch == own).astype(BF16)
            return carry

        lax.fori_loop(0, regions * steps, build, 0)

    def smoothed(pair):
        wide = jnp.concatenate([along_lon(x, lon_ref[...]) for x in pair], axis=1)
        return along_lat(wide, lat_ref[...], wide)

    every = regions * rows
    for device in range(devices):
        pair = [
            jnp.concatenate(
                [field_ref[region * devices + device, 0, k] for region in range(regions)], axis=0
            )
            for k in range(held)
        ]
        result = smoothed(pair)
        for k in range(held):
            cells[pl.ds(device * held + k, every, stride=members), :] = result[
                :, k * lon : (k + 1) * lon
            ]

    for region in range(regions):
        own_truth = lax.rem(me_ref[0] - region + regions, regions)

        def load(step, j):
            row = step * STEP + j
            start = pl.multiple_of((region * rows + row) * members, members)
            a = cells[pl.ds(start, members), :]
            return start, a, a - truth_ref[own_truth, 0, pl.ds(row, 1), :]

        def first(step, total):
            columns = []
            for j in range(STEP):
                _, a, miss = load(step, j)
                gaps = [a - pltpu.roll(a, s, 0) for s in range(1, shifts + 1)] + [miss]
                columns.append(jnp.concatenate([gap * gap for gap in gaps], axis=0))
            squares = jnp.concatenate(columns, axis=1)
            return total + patch_sums(squares, hots[region * steps + step])

        height = (shifts + 1) * members
        total = lax.fori_loop(0, steps, first, jnp.zeros((2 * height, patches), F32))
        weights = lax.rsqrt(total[:height] + total[height:] + EPS)
        factor = jnp.where(
            lax.broadcasted_iota(jnp.int32, (height, patches), 0) < shifts * members,
            -scale / members,
            scale,
        )
        weights = head_and_tail(weights * factor)

        def second(step, carry):
            spread = on_cells(weights, hots[region * steps + step])
            for j in range(STEP):
                start, a, miss = load(step, j)
                w = spread[:, j * lon : (j + 1) * lon]
                h = w[shifts * members :] * miss
                for s in range(1, shifts + 1):
                    pull = w[(s - 1) * members : s * members] * (a - pltpu.roll(a, s, 0))
                    h = h + pull
                    if 2 * s != members:
                        h = h - pltpu.roll(pull, members - s, 0)
                cells[pl.ds(start, members), :] = h
            return carry

        lax.fori_loop(0, steps, second, 0)

    for device in range(devices):
        result = smoothed(
            [cells[pl.ds(device * held + k, every, stride=members), :] for k in range(held)]
        )
        for region in range(regions):
            for k in range(held):
                out_ref[region * devices + device, 0, k] = result[
                    region * rows : (region + 1) * rows, k * lon : (k + 1) * lon
                ]


def whole_fields(fields, truth, patch_map, regions):
    sources, count, held, rows, lon = fields.shape
    members = sources // regions * held
    patches = rows * lon // PATCH
    every = regions * rows
    me = lax.axis_index("region").reshape(1)
    block = pl.BlockSpec((sources, 1, held, rows, lon), lambda v, me: (0, v, 0, 0, 0))
    pairs = every * lon * members * (members // 2 + 1)
    return pl.pallas_call(
        functools.partial(field_kernel, regions),
        out_shape=jax.ShapeDtypeStruct(fields.shape, F32),
        grid_spec=pltpu.PrefetchScalarGridSpec(
            num_scalar_prefetch=1,
            grid=(count,),
            in_specs=[
                block,
                pl.BlockSpec((regions, 1, rows, lon), lambda v, me: (0, v, 0, 0)),
                pl.BlockSpec((every, lon), lambda v, me: (0, 0)),
                pl.BlockSpec((3 * lon, lon), lambda v, me: (0, 0)),
                pl.BlockSpec((every, 3 * every), lambda v, me: (0, 0)),
            ],
            out_specs=block,
            scratch_shapes=[
                pltpu.VMEM((every * members, lon), F32),
                pltpu.VMEM((every // STEP, patches, STEP * lon), BF16),
            ],
        ),
        compiler_params=pltpu.CompilerParams(vmem_limit_bytes=VMEM),
        cost_estimate=pl.CostEstimate(
            flops=count * pairs * patches * 8, bytes_accessed=8 * fields.size, transcendentals=0
        ),
        name="whole_fields",
    )(me, fields, truth, patch_map, lon_weights(lon), lat_weights(every, 0))


def smooth_kernel(own_ref, low_ref, high_ref, lon_ref, lat_ref, out_ref):
    held = own_ref.shape[0]
    for k in range(held):
        rows = [ref[k, 0] for ref in (low_ref, own_ref, high_ref)]
        wide = along_lon(jnp.concatenate(rows, axis=0), lon_ref[...])
        pad = rows[0].shape[0]
        out_ref[k, 0] = along_lat(wide, lat_ref[...], wide[pad : pad + rows[1].shape[0]])


def smoothed_rows(own):
    held, count, rows, lon = own.shape
    regions = lax.axis_size("region")
    up = [(i, i + 1) for i in range(regions - 1)]
    low = lax.ppermute(own[:, :, rows - HALF :], "region", up)
    high = lax.ppermute(own[:, :, :HALF], "region", [(b, a) for a, b in up])
    edge = pl.BlockSpec((held, 1, HALF, lon), lambda v: (0, v, 0, 0))
    block = pl.BlockSpec((held, 1, rows, lon), lambda v: (0, v, 0, 0))
    span = rows + 2 * HALF
    return pl.pallas_call(
        smooth_kernel,
        out_shape=jax.ShapeDtypeStruct(own.shape, F32),
        grid=(count,),
        in_specs=[
            block,
            edge,
            edge,
            pl.BlockSpec((3 * lon, lon), lambda v: (0, 0)),
            pl.BlockSpec((rows, 3 * span), lambda v: (0, 0)),
        ],
        out_specs=block,
        compiler_params=pltpu.CompilerParams(vmem_limit_bytes=VMEM),
        name="smoothed_rows",
    )(own, low, high, lon_weights(lon), lat_weights(rows, HALF))


def share_kernel(all_ref, own_ref, truth_ref, map_ref, out_ref, cells, hots):
    devices, held, _, rows, lon = all_ref.shape
    members = devices * held
    patches = hots.shape[1]
    scale = float(np.sqrt(PATCH))
    steps = rows // STEP

    @pl.when(pl.program_id(0) == 0)
    def _():
        patch = lax.broadcasted_iota(jnp.int32, (patches, lon), 0).astype(F32)
        for row in range(rows):
            hots[row // STEP, :, row % STEP * lon : (row % STEP + 1) * lon] = (
                patch == map_ref[row : row + 1, :]
            ).astype(BF16)

    for device in range(devices):
        for k in range(held):
            cells[pl.ds(device * held + k, rows, stride=members), :] = all_ref[device, k, 0]

    def gaps(step, j):
        row = step * STEP + j
        a = cells[pl.ds(pl.multiple_of(row * members, members), members), :]
        truth = truth_ref[0, pl.ds(row, 1), :]
        result = []
        for k in range(held):
            own = own_ref[k, 0, pl.ds(row, 1), :]
            result += [own - a, jnp.broadcast_to(own - truth, (8, lon))]
        return row, result

    def first(step, total):
        columns = [
            jnp.concatenate([gap * gap for gap in gaps(step, j)[1]], axis=0) for j in range(STEP)
        ]
        return total + patch_sums(jnp.concatenate(columns, axis=1), hots[step])

    height = held * (members + 8)
    total = lax.fori_loop(0, steps, first, jnp.zeros((2 * height, patches), F32))
    weights = lax.rsqrt(total[:height] + total[height:] + EPS)
    place = lax.rem(lax.broadcasted_iota(jnp.int32, (height, patches), 0), members + 8)
    weights = head_and_tail(weights * jnp.where(place < members, -scale / members, scale))

    def second(step, carry):
        spread = on_cells(weights, hots[step])
        for j in range(STEP):
            row, parts = gaps(step, j)
            w = spread[:, j * lon : (j + 1) * lon]
            for k in range(held):
                base = k * (members + 8)
                pull = w[base : base + members] * parts[2 * k]
                toward = w[base + members : base + members + 1] * parts[2 * k + 1][:1]
                out_ref[k, 0, pl.ds(row, 1), :] = toward + jnp.sum(pull, axis=0, keepdims=True)
        return carry

    lax.fori_loop(0, steps, second, 0)


def own_members(smooth, truth, patch_map):
    held, count, rows, lon = smooth.shape
    devices = lax.axis_size("member")
    patches = rows * lon // PATCH
    everyone = lax.all_gather(smooth, "member")
    block = pl.BlockSpec((held, 1, rows, lon), lambda v: (0, v, 0, 0))
    return pl.pallas_call(
        share_kernel,
        out_shape=jax.ShapeDtypeStruct(smooth.shape, F32),
        grid=(count,),
        in_specs=[
            pl.BlockSpec((devices, held, 1, rows, lon), lambda v: (0, 0, v, 0, 0)),
            block,
            pl.BlockSpec((1, rows, lon), lambda v: (v, 0, 0)),
            pl.BlockSpec((rows, lon), lambda v: (0, 0)),
        ],
        out_specs=block,
        scratch_shapes=[
            pltpu.VMEM((rows * devices * held, lon), F32),
            pltpu.VMEM((rows // STEP, patches, STEP * lon), BF16),
        ],
        compiler_params=pltpu.CompilerParams(vmem_limit_bytes=VMEM),
        name="own_members",
    )(everyone, smooth, truth, patch_map)


def patch_of_cell(order, rows, lon):
    position = jnp.arange(rows * lon, dtype=jnp.int32)
    in_row = jnp.arange(rows, dtype=jnp.int32)[:, None] == (order // lon)[None]
    at_lon = (order % lon)[:, None] == jnp.arange(lon, dtype=jnp.int32)[None]
    patch = jnp.where(in_row, (position // PATCH)[None], 0)
    return jnp.dot(
        patch.astype(F32), at_lon.astype(F32), precision=lax.Precision.HIGHEST
    )


def on_device(predicted_states, observed_analysis, tile_location_sequence):
    held, variables, rows, lon = predicted_states.shape
    regions, devices = lax.axis_size("region"), lax.axis_size("member")
    total = regions * devices
    share = variables // total
    whole = share * total
    patch_map = patch_of_cell(tile_location_sequence[0], rows, lon)
    parts = []
    if share:
        region, member = lax.axis_index("region"), lax.axis_index("member")
        maps = lax.all_gather(patch_map, "region").reshape(regions * rows, lon)
        truth = []
        for shift in range(regions):
            owner = lax.rem(region + shift, regions) * devices + member
            piece = lax.dynamic_slice_in_dim(observed_analysis, owner * share, share, axis=0)
            if shift:
                piece = lax.ppermute(
                    piece, "region", [(i, (i + shift) % regions) for i in range(regions)]
                )
            truth.append(piece)
        truth = jnp.stack(truth)
        sent = predicted_states[:, :whole].reshape(held, total, share, rows, lon)
        fields = lax.all_to_all(
            jnp.transpose(sent, (1, 2, 0, 3, 4)), ("region", "member"), 0, 0, tiled=True
        )
        result = whole_fields(fields, truth, maps, regions)
        result = lax.all_to_all(result, ("region", "member"), 0, 0, tiled=True)
        parts.append(jnp.transpose(result, (2, 0, 1, 3, 4)).reshape(held, whole, rows, lon))
    if whole < variables:
        smooth = smoothed_rows(predicted_states[:, whole:])
        h = own_members(smooth, observed_analysis[whole:], patch_map)
        parts.append(smoothed_rows(h))
    return jnp.concatenate(parts, axis=1)


def solution(mesh):
    in_specs = (P("member", None, "region", None), P(None, "region", None), P("region", None))
    out_specs = P("member", None, "region", None)
    return jax.shard_map(
        on_device, mesh=mesh, in_specs=in_specs, out_specs=out_specs, check_vma=False
    )
```

```python
import functools

import jax
import jax.numpy as jnp
import numpy as np
from jax import lax
from jax.experimental import pallas as pl
from jax.experimental.pallas import tpu as pltpu
from jax.sharding import PartitionSpec as P

HALF = 32
PATCH = 128
EPS = 1e-06
STEP = 32
BLOCK = 8
VMEM = 56 * 1024 * 1024
F32 = jnp.float32
BF16 = jnp.bfloat16


def bell(out_cells, in_cells):
    sigma = HALF / 2.0
    steps = np.arange(-HALF, HALF + 1)
    norm = np.sum(np.exp(-(steps**2) / (2.0 * sigma**2)))
    offset = np.asarray(in_cells)[None, :] - np.asarray(out_cells)[:, None]
    value = 0.5 * np.exp(-(offset**2) / (2.0 * sigma**2)) / norm
    value = jnp.asarray(np.where(np.abs(offset) <= HALF, value, 0.0), F32)
    return halves(value)


def halves(x):
    head = x.astype(BF16)
    return head, (x - head.astype(F32)).astype(BF16)


def lon_weights(lon):
    head, tail = bell(range(lon), range(lon))
    return jnp.concatenate([head, head, tail], axis=0)


def lat_weights(rows, pad):
    head, tail = bell(range(rows), range(-pad, rows + pad))
    return jnp.concatenate([head, head, tail], axis=1)


def along_lon(x, weights):
    head, tail = halves(x)
    return 0.5 * x + jnp.dot(
        jnp.concatenate([head, tail, head], axis=1), weights, preferred_element_type=F32
    )


def along_lat(x, weights, own):
    head, tail = halves(x)
    return 0.5 * own + jnp.dot(
        weights, jnp.concatenate([head, tail, head], axis=0), preferred_element_type=F32
    )


def patch_sums(squares, hot):
    return lax.dot_general(
        squares,
        hot,
        (((1,), (1,)), ((), ())),
        preferred_element_type=F32,
    )


def on_cells(weights, hot):
    return jnp.dot(weights, jnp.concatenate([hot, hot], axis=0), preferred_element_type=F32)


def head_and_tail(weights):
    return jnp.concatenate(halves(weights), axis=1)


def member_gaps(blocks):
    gaps = [x - pltpu.roll(x, s, 0) for x in blocks for s in range(1, BLOCK // 2 + 1)]
    for b, x in enumerate(blocks):
        for y in blocks[b + 1 :]:
            gaps.append(x - y)
            gaps += [x - pltpu.roll(y, s, 0) for s in range(1, BLOCK)]
    return gaps


def member_pulls(pulls, count):
    pulls = iter(pulls)
    sums = [0.0] * count
    for b in range(count):
        for s in range(1, BLOCK // 2 + 1):
            pull = next(pulls)
            sums[b] = sums[b] + pull
            if 2 * s != BLOCK:
                sums[b] = sums[b] - pltpu.roll(pull, BLOCK - s, 0)
    for b in range(count):
        for c in range(b + 1, count):
            for s in range(BLOCK):
                pull = next(pulls)
                sums[b] = sums[b] + pull
                sums[c] = sums[c] - (pltpu.roll(pull, BLOCK - s, 0) if s else pull)
    return sums


def field_kernel(
    regions, me_ref, field_ref, truth_ref, map_ref, lon_ref, lat_ref, out_ref, cells, hots
):
    sources, _, lon = field_ref.shape
    rows = truth_ref.shape[2]
    held = field_ref.shape[1] // rows
    devices = sources // regions
    members = devices * held
    blocks = members // BLOCK
    pairs = blocks * (BLOCK // 2) + blocks * (blocks - 1) // 2 * BLOCK
    height = (pairs + blocks) * BLOCK
    steps = rows // STEP
    patches = hots.shape[1]
    scale = float(np.sqrt(PATCH))

    def shift_of(region):
        return lax.rem(me_ref[0] - region + regions, regions)

    @pl.when(pl.program_id(0) == 0)
    def _():
        patch = lax.broadcasted_iota(jnp.int32, (patches, lon), 0).astype(F32)

        def build(block, carry):
            for j in range(STEP):
                own = map_ref[shift_of(block // steps), 0, pl.ds(block % steps * STEP + j, 1), :]
                hots[block, :, j * lon : (j + 1) * lon] = (patch == own).astype(BF16)
            return carry

        lax.fori_loop(0, regions * steps, build, 0)

    def smoothed(pair):
        wide = jnp.concatenate([along_lon(x, lon_ref[...]) for x in pair], axis=1)
        return along_lat(wide, lat_ref[...], wide)

    every = regions * rows
    for device in range(devices):
        pair = [
            jnp.concatenate(
                [
                    field_ref[region * devices + device, k * rows : (k + 1) * rows, :]
                    for region in range(regions)
                ],
                axis=0,
            )
            for k in range(held)
        ]
        result = smoothed(pair)
        for k in range(held):
            cells[pl.ds(device * held + k, every, stride=members), :] = result[
                :, k * lon : (k + 1) * lon
            ]

    for region in range(regions):
        shift = shift_of(region)

        def load(row):
            start = pl.multiple_of((region * rows + row) * members, members)
            a = [cells[pl.ds(start + b * BLOCK, BLOCK), :] for b in range(blocks)]
            truth = truth_ref[shift, 0, pl.ds(row, 1), :]
            return start, member_gaps(a) + [x - truth for x in a]

        def first(step, total):
            heads, tails = [], []
            for j in range(STEP):
                head, tail = halves(
                    jnp.concatenate([gap * gap for gap in load(step * STEP + j)[1]], axis=0)
                )
                heads.append(head)
                tails.append(tail)
            squares = jnp.concatenate(
                [jnp.concatenate(heads, axis=1), jnp.concatenate(tails, axis=1)], axis=0
            )
            return total + patch_sums(squares, hots[region * steps + step])

        total = lax.fori_loop(0, steps, first, jnp.zeros((2 * height, patches), F32))
        weights = lax.rsqrt(total[:height] + total[height:] + EPS)
        factor = jnp.where(
            lax.broadcasted_iota(jnp.int32, (height, patches), 0) < pairs * BLOCK,
            -scale / members,
            scale,
        )
        weights = head_and_tail(weights * factor)

        def second(step, carry):
            spread = on_cells(weights, hots[region * steps + step])
            for j in range(STEP):
                start, gaps = load(step * STEP + j)
                w = spread[:, j * lon : (j + 1) * lon]
                terms = [w[i * BLOCK : (i + 1) * BLOCK] * gap for i, gap in enumerate(gaps)]
                sums = member_pulls(terms[:pairs], blocks)
                for b in range(blocks):
                    cells[pl.ds(start + b * BLOCK, BLOCK), :] = sums[b] + terms[pairs + b]
            return carry

        lax.fori_loop(0, steps, second, 0)

    for device in range(devices):
        result = smoothed(
            [cells[pl.ds(device * held + k, every, stride=members), :] for k in range(held)]
        )
        for region in range(regions):
            for k in range(held):
                out_ref[region * devices + device, k * rows : (k + 1) * rows, :] = result[
                    region * rows : (region + 1) * rows, k * lon : (k + 1) * lon
                ]


def whole_fields(fields, count, held, extra, offset):
    sources, _, lon = fields.shape
    regions, variables, rows, _ = extra.shape
    members = sources // regions * held
    patches = rows * lon // PATCH
    every = regions * rows
    me = lax.axis_index("region").reshape(1)
    block = pl.BlockSpec((sources, held * rows, lon), lambda v, me: (0, v, 0))
    pairs = every * lon * members * (members // 2 + 1)
    return pl.pallas_call(
        functools.partial(field_kernel, regions),
        out_shape=jax.ShapeDtypeStruct((sources, count * held * rows, lon), F32),
        grid_spec=pltpu.PrefetchScalarGridSpec(
            num_scalar_prefetch=1,
            grid=(count,),
            in_specs=[
                block,
                pl.BlockSpec((regions, 1, rows, lon), lambda v, me: (0, v + offset, 0, 0)),
                pl.BlockSpec((regions, 1, rows, lon), lambda v, me: (0, variables - 1, 0, 0)),
                pl.BlockSpec((3 * lon, lon), lambda v, me: (0, 0)),
                pl.BlockSpec((every, 3 * every), lambda v, me: (0, 0)),
            ],
            out_specs=block,
            scratch_shapes=[
                pltpu.VMEM((every * members, lon), F32),
                pltpu.VMEM((every // STEP, patches, STEP * lon), BF16),
            ],
        ),
        compiler_params=pltpu.CompilerParams(vmem_limit_bytes=VMEM),
        cost_estimate=pl.CostEstimate(
            flops=count * pairs * patches * 8,
            bytes_accessed=8 * count * every * lon * members,
            transcendentals=0,
        ),
        name="whole_fields",
    )(me, fields, extra, extra, lon_weights(lon), lat_weights(every, 0))


def smooth_kernel(own_ref, low_ref, high_ref, lon_ref, lat_ref, out_ref):
    held = own_ref.shape[0]
    for k in range(held):
        rows = [ref[k, 0] for ref in (low_ref, own_ref, high_ref)]
        wide = along_lon(jnp.concatenate(rows, axis=0), lon_ref[...])
        pad = rows[0].shape[0]
        out_ref[k, 0] = along_lat(wide, lat_ref[...], wide[pad : pad + rows[1].shape[0]])


def smoothed_rows(own):
    held, count, rows, lon = own.shape
    regions = lax.axis_size("region")
    up = [(i, i + 1) for i in range(regions - 1)]
    low = lax.ppermute(own[:, :, rows - HALF :], "region", up)
    high = lax.ppermute(own[:, :, :HALF], "region", [(b, a) for a, b in up])
    edge = pl.BlockSpec((held, 1, HALF, lon), lambda v: (0, v, 0, 0))
    block = pl.BlockSpec((held, 1, rows, lon), lambda v: (0, v, 0, 0))
    span = rows + 2 * HALF
    return pl.pallas_call(
        smooth_kernel,
        out_shape=jax.ShapeDtypeStruct(own.shape, F32),
        grid=(count,),
        in_specs=[
            block,
            edge,
            edge,
            pl.BlockSpec((3 * lon, lon), lambda v: (0, 0)),
            pl.BlockSpec((rows, 3 * span), lambda v: (0, 0)),
        ],
        out_specs=block,
        compiler_params=pltpu.CompilerParams(vmem_limit_bytes=VMEM),
        name="smoothed_rows",
    )(own, low, high, lon_weights(lon), lat_weights(rows, HALF))


def share_kernel(all_ref, own_ref, truth_ref, map_ref, out_ref, cells, hots):
    devices, held, _, rows, lon = all_ref.shape
    members = devices * held
    patches = hots.shape[1]
    scale = float(np.sqrt(PATCH))
    steps = rows // STEP

    @pl.when(pl.program_id(0) == 0)
    def _():
        patch = lax.broadcasted_iota(jnp.int32, (patches, lon), 0).astype(F32)
        for row in range(rows):
            hots[row // STEP, :, row % STEP * lon : (row % STEP + 1) * lon] = (
                patch == map_ref[row : row + 1, :]
            ).astype(BF16)

    for device in range(devices):
        for k in range(held):
            cells[pl.ds(device * held + k, rows, stride=members), :] = all_ref[device, k, 0]

    def gaps(step, j):
        row = step * STEP + j
        a = cells[pl.ds(pl.multiple_of(row * members, members), members), :]
        truth = truth_ref[0, pl.ds(row, 1), :]
        result = []
        for k in range(held):
            own = own_ref[k, 0, pl.ds(row, 1), :]
            result += [own - a, jnp.broadcast_to(own - truth, (8, lon))]
        return row, result

    def first(step, total):
        columns = [
            jnp.concatenate([gap * gap for gap in gaps(step, j)[1]], axis=0) for j in range(STEP)
        ]
        squares = jnp.concatenate(halves(jnp.concatenate(columns, axis=1)), axis=0)
        return total + patch_sums(squares, hots[step])

    height = held * (members + 8)
    total = lax.fori_loop(0, steps, first, jnp.zeros((2 * height, patches), F32))
    weights = lax.rsqrt(total[:height] + total[height:] + EPS)
    place = lax.rem(lax.broadcasted_iota(jnp.int32, (height, patches), 0), members + 8)
    weights = head_and_tail(weights * jnp.where(place < members, -scale / members, scale))

    def second(step, carry):
        spread = on_cells(weights, hots[step])
        for j in range(STEP):
            row, parts = gaps(step, j)
            w = spread[:, j * lon : (j + 1) * lon]
            for k in range(held):
                base = k * (members + 8)
                pull = w[base : base + members] * parts[2 * k]
                toward = w[base + members : base + members + 1] * parts[2 * k + 1][:1]
                out_ref[k, 0, pl.ds(row, 1), :] = toward + jnp.sum(pull, axis=0, keepdims=True)
        return carry

    lax.fori_loop(0, steps, second, 0)


def own_members(everyone, smooth, truth, patch_map):
    held, count, rows, lon = smooth.shape
    devices = everyone.shape[0]
    patches = rows * lon // PATCH
    block = pl.BlockSpec((held, 1, rows, lon), lambda v: (0, v, 0, 0))
    return pl.pallas_call(
        share_kernel,
        out_shape=jax.ShapeDtypeStruct(smooth.shape, F32),
        grid=(count,),
        in_specs=[
            pl.BlockSpec((devices, held, 1, rows, lon), lambda v: (0, 0, v, 0, 0)),
            block,
            pl.BlockSpec((1, rows, lon), lambda v: (v, 0, 0)),
            pl.BlockSpec((rows, lon), lambda v: (0, 0)),
        ],
        out_specs=block,
        scratch_shapes=[
            pltpu.VMEM((rows * devices * held, lon), F32),
            pltpu.VMEM((rows // STEP, patches, STEP * lon), BF16),
        ],
        compiler_params=pltpu.CompilerParams(vmem_limit_bytes=VMEM),
        name="own_members",
    )(everyone, smooth, truth, patch_map)


def patch_of_cell(order, rows, lon):
    position = jnp.arange(rows * lon, dtype=jnp.int32)
    in_row = jnp.arange(rows, dtype=jnp.int32)[:, None] == (order // lon)[None]
    at_lon = (order % lon)[:, None] == jnp.arange(lon, dtype=jnp.int32)[None]
    patch = jnp.where(in_row, (position // PATCH)[None], 0)
    return jnp.dot(
        patch.astype(F32), at_lon.astype(F32), precision=lax.Precision.HIGHEST
    )


def exchange(blocks):
    return lax.all_to_all(blocks, ("region", "member"), 0, 0, tiled=True)


def sent_rows(x, count):
    held, variables, rows, lon = x.shape
    total = variables // count
    x = jnp.transpose(x.reshape(held, total, count, rows, lon), (1, 2, 0, 3, 4))
    return x.reshape(total, count * held * rows, lon)


def kept_rows(blocks, held, rows):
    total, height, lon = blocks.shape
    count = height // (held * rows)
    x = blocks.reshape(total, count, held, rows, lon)
    return jnp.transpose(x, (2, 0, 1, 3, 4)).reshape(held, total * count, rows, lon)


def is_power(n):
    return n & (n - 1) == 0


def sent_pieces(x, regions, devices):
    held, variables, rows, lon = x.shape
    near = devices // variables
    x = x.reshape(held, variables, regions, near, rows // (regions * near), lon)
    x = jnp.transpose(x, (2, 1, 3, 0, 4, 5))
    return x.reshape(regions * devices, -1, lon)


def kept_pieces(blocks, held, variables, regions, devices):
    near = devices // variables
    lon = blocks.shape[-1]
    x = blocks.reshape(regions, variables, near, held, -1, lon)
    return jnp.transpose(x, (3, 1, 0, 2, 4, 5)).reshape(held, variables, -1, lon)


def plane_gather(x, near, beside):
    x = x[None]
    for axis, size in (("member", near), ("region", lax.axis_size("region"))):
        index, step = lax.axis_index(axis), 1
        while step < size:
            count = lax.axis_size(axis)
            other = lax.ppermute(x, axis, [(i, i ^ step) for i in range(count)])
            if beside is not None:
                other, beside = lax.optimization_barrier((other, beside))
                result, beside = beside, None
            low = (index & step) == 0
            x = jnp.concatenate([jnp.where(low, x, other), jnp.where(low, other, x)], axis=0)
            step *= 2
    return x, result


def extras(observed, patch_map, starts, counts):
    regions = lax.axis_size("region")
    region, member = lax.axis_index("region"), lax.axis_index("member")
    result = []
    for shift in range(regions):
        owner = lax.rem(region + shift, regions), member
        pieces = [
            lax.dynamic_slice_in_dim(observed, start(*owner), count, axis=0)
            for start, count in zip(starts, counts)
        ]
        piece = jnp.concatenate(pieces + [patch_map[None]], axis=0)
        if shift:
            ring = [(i, (i + shift) % regions) for i in range(regions)]
            piece = lax.ppermute(piece, "region", ring)
        result.append(piece)
    return jnp.stack(result)


def spread_over_all(forecast, observed, patch_map):
    held, variables, rows, lon = forecast.shape
    regions, devices = lax.axis_size("region"), lax.axis_size("member")
    region, member = lax.axis_index("region"), lax.axis_index("member")
    total = regions * devices
    share = variables // total
    chunks = [count for count in (share // 2, share - share // 2) if count]
    left = variables - share * total
    sent, starts, counts, begin = [], [], [], 0
    for count in chunks:
        sent.append(sent_rows(forecast[:, begin : begin + count * total], count))
        starts.append(lambda r, m, b=begin, c=count: b + (r * devices + m) * c)
        counts.append(count)
        begin += count * total
    if left:
        near = devices // left
        sent[0] = jnp.concatenate(
            [sent[0], sent_pieces(forecast[:, begin:], regions, devices)], axis=1
        )
        starts.append(lambda r, m, b=begin: b + m // near)
        counts.append(1)
    extra = extras(observed, patch_map, starts, counts)
    if len(chunks) > 1:
        sent[1:], extra = lax.optimization_barrier((sent[1:], extra))
    fields = [exchange(part) for part in sent]
    results = [
        whole_fields(field, count, held, extra, sum(chunks[:i]))
        for i, (field, count) in enumerate(zip(fields, chunks))
    ]
    body = chunks[0] * held * rows
    if left:
        piece = rows // (regions * near)
        field, results[0] = plane_gather(fields[0][:, body:], near, results[0])
        field = field.reshape(-1, total, held, piece, lon)
        field = jnp.transpose(field, (1, 2, 0, 3, 4)).reshape(total, held * rows, lon)
        result = whole_fields(field, 1, held, extra, share).reshape(total, held, rows, lon)
        place = region * near + lax.rem(member, near)
        result = lax.dynamic_slice_in_dim(result, place * piece, piece, axis=2)
        results[0] = jnp.concatenate([results[0], result.reshape(total, -1, lon)], axis=1)
    backs = [exchange(result) for result in results]
    parts = [kept_rows(back[:, : count * held * rows], held, rows) for back, count in zip(backs, chunks)]
    if left:
        parts.append(kept_pieces(backs[0][:, body:], held, left, regions, devices))
    return jnp.concatenate(parts, axis=1)


def on_device(predicted_states, observed_analysis, tile_location_sequence):
    _, variables, rows, lon = predicted_states.shape
    regions, devices = lax.axis_size("region"), lax.axis_size("member")
    patch_map = patch_of_cell(tile_location_sequence[0], rows, lon)
    left = variables % (regions * devices)
    planes = left == 0 or (
        devices % left == 0
        and rows % (regions * devices // left) == 0
        and is_power(regions)
        and is_power(devices // left)
    )
    if variables >= regions * devices and planes:
        return spread_over_all(predicted_states, observed_analysis, patch_map)
    smooth = smoothed_rows(predicted_states)
    everyone = lax.all_gather(smooth, "member")
    return smoothed_rows(own_members(everyone, smooth, observed_analysis, patch_map))


def solution(mesh):
    in_specs = (P("member", None, "region", None), P(None, "region", None), P("region", None))
    out_specs = P("member", None, "region", None)
    return jax.shard_map(
        on_device, mesh=mesh, in_specs=in_specs, out_specs=out_specs, check_vma=False
    )
```

```python
import functools

import jax
import jax.numpy as jnp
import numpy as np
from jax import lax
from jax.experimental import pallas as pl
from jax.experimental.pallas import tpu as pltpu
from jax.sharding import PartitionSpec as P

HALF = 32
PATCH = 128
EPS = 1e-06
STEP = 32
BLOCK = 8
VMEM = 56 * 1024 * 1024
F32 = jnp.float32
BF16 = jnp.bfloat16


def bell(out_cells, in_cells):
    sigma = HALF / 2.0
    steps = np.arange(-HALF, HALF + 1)
    norm = np.sum(np.exp(-(steps**2) / (2.0 * sigma**2)))
    offset = np.asarray(in_cells)[None, :] - np.asarray(out_cells)[:, None]
    value = 0.5 * np.exp(-(offset**2) / (2.0 * sigma**2)) / norm
    value = jnp.asarray(np.where(np.abs(offset) <= HALF, value, 0.0), F32)
    return halves(value)


def halves(x):
    head = x.astype(BF16)
    return head, (x - head.astype(F32)).astype(BF16)


def lon_weights(lon):
    head, tail = bell(range(lon), range(lon))
    return jnp.concatenate([head, head, tail], axis=0)


def lat_weights(rows, pad):
    head, tail = bell(range(rows), range(-pad, rows + pad))
    return jnp.concatenate([head, head, tail], axis=1)


def along_lon(x, weights):
    head, tail = halves(x)
    return 0.5 * x + jnp.dot(
        jnp.concatenate([head, tail, head], axis=1), weights, preferred_element_type=F32
    )


def along_lat(x, weights, own):
    head, tail = halves(x)
    return 0.5 * own + jnp.dot(
        weights, jnp.concatenate([head, tail, head], axis=0), preferred_element_type=F32
    )


def patch_sums(squares, hot):
    return lax.dot_general(
        squares,
        hot,
        (((1,), (1,)), ((), ())),
        preferred_element_type=F32,
    )


def on_cells(weights, hot):
    return jnp.dot(weights, jnp.concatenate([hot, hot], axis=0), preferred_element_type=F32)


def head_and_tail(weights):
    return jnp.concatenate(halves(weights), axis=1)


def member_gaps(blocks):
    gaps = [x - pltpu.roll(x, s, 0) for x in blocks for s in range(1, BLOCK // 2 + 1)]
    for b, x in enumerate(blocks):
        for y in blocks[b + 1 :]:
            gaps.append(x - y)
            gaps += [x - pltpu.roll(y, s, 0) for s in range(1, BLOCK)]
    return gaps


def member_pulls(pulls, count):
    pulls = iter(pulls)
    sums = [0.0] * count
    for b in range(count):
        for s in range(1, BLOCK // 2 + 1):
            pull = next(pulls)
            sums[b] = sums[b] + pull
            if 2 * s != BLOCK:
                sums[b] = sums[b] - pltpu.roll(pull, BLOCK - s, 0)
    for b in range(count):
        for c in range(b + 1, count):
            for s in range(BLOCK):
                pull = next(pulls)
                sums[b] = sums[b] + pull
                sums[c] = sums[c] - (pltpu.roll(pull, BLOCK - s, 0) if s else pull)
    return sums


def field_kernel(
    regions, me_ref, field_ref, truth_ref, map_ref, lon_ref, lat_ref, out_ref, cells, hots
):
    sources, _, lon = field_ref.shape
    rows = truth_ref.shape[2]
    held = field_ref.shape[1] // rows
    devices = sources // regions
    members = devices * held
    blocks = members // BLOCK
    pairs = blocks * (BLOCK // 2) + blocks * (blocks - 1) // 2 * BLOCK
    height = (pairs + blocks) * BLOCK
    steps = rows // STEP
    patches = hots.shape[1]
    scale = float(np.sqrt(PATCH))

    def shift_of(region):
        return lax.rem(me_ref[0] - region + regions, regions)

    @pl.when(pl.program_id(0) == 0)
    def _():
        patch = lax.broadcasted_iota(jnp.int32, (patches, lon), 0).astype(F32)

        def build(block, carry):
            for j in range(STEP):
                own = map_ref[shift_of(block // steps), 0, pl.ds(block % steps * STEP + j, 1), :]
                hots[block, :, j * lon : (j + 1) * lon] = (patch == own).astype(BF16)
            return carry

        lax.fori_loop(0, regions * steps, build, 0)

    def smoothed(pair):
        wide = jnp.concatenate([along_lon(x, lon_ref[...]) for x in pair], axis=1)
        return along_lat(wide, lat_ref[...], wide)

    every = regions * rows
    for device in range(devices):
        pair = [
            jnp.concatenate(
                [
                    field_ref[region * devices + device, k * rows : (k + 1) * rows, :]
                    for region in range(regions)
                ],
                axis=0,
            )
            for k in range(held)
        ]
        result = smoothed(pair)
        for k in range(held):
            cells[pl.ds(device * held + k, every, stride=members), :] = result[
                :, k * lon : (k + 1) * lon
            ]

    for region in range(regions):
        shift = shift_of(region)

        def load(row):
            start = pl.multiple_of((region * rows + row) * members, members)
            a = [cells[pl.ds(start + b * BLOCK, BLOCK), :] for b in range(blocks)]
            truth = truth_ref[shift, 0, pl.ds(row, 1), :]
            return start, member_gaps(a) + [x - truth for x in a]

        def first(step, total):
            heads, tails = [], []
            for j in range(STEP):
                head, tail = halves(
                    jnp.concatenate([gap * gap for gap in load(step * STEP + j)[1]], axis=0)
                )
                heads.append(head)
                tails.append(tail)
            squares = jnp.concatenate(
                [jnp.concatenate(heads, axis=1), jnp.concatenate(tails, axis=1)], axis=0
            )
            return total + patch_sums(squares, hots[region * steps + step])

        total = lax.fori_loop(0, steps, first, jnp.zeros((2 * height, patches), F32))
        weights = lax.rsqrt(total[:height] + total[height:] + EPS)
        factor = jnp.where(
            lax.broadcasted_iota(jnp.int32, (height, patches), 0) < pairs * BLOCK,
            -scale / members,
            scale,
        )
        weights = head_and_tail(weights * factor)

        def second(step, carry):
            spread = on_cells(weights, hots[region * steps + step])
            for j in range(STEP):
                start, gaps = load(step * STEP + j)
                w = spread[:, j * lon : (j + 1) * lon]
                terms = [w[i * BLOCK : (i + 1) * BLOCK] * gap for i, gap in enumerate(gaps)]
                sums = member_pulls(terms[:pairs], blocks)
                for b in range(blocks):
                    cells[pl.ds(start + b * BLOCK, BLOCK), :] = sums[b] + terms[pairs + b]
            return carry

        lax.fori_loop(0, steps, second, 0)

    for device in range(devices):
        result = smoothed(
            [cells[pl.ds(device * held + k, every, stride=members), :] for k in range(held)]
        )
        for region in range(regions):
            for k in range(held):
                out_ref[region * devices + device, k * rows : (k + 1) * rows, :] = result[
                    region * rows : (region + 1) * rows, k * lon : (k + 1) * lon
                ]


def whole_fields(fields, count, held, extra, offset):
    sources, _, lon = fields.shape
    regions, variables, rows, _ = extra.shape
    members = sources // regions * held
    patches = rows * lon // PATCH
    every = regions * rows
    me = lax.axis_index("region").reshape(1)
    block = pl.BlockSpec((sources, held * rows, lon), lambda v, me: (0, v, 0))
    pairs = every * lon * members * (members // 2 + 1)
    return pl.pallas_call(
        functools.partial(field_kernel, regions),
        out_shape=jax.ShapeDtypeStruct((sources, count * held * rows, lon), F32),
        grid_spec=pltpu.PrefetchScalarGridSpec(
            num_scalar_prefetch=1,
            grid=(count,),
            in_specs=[
                block,
                pl.BlockSpec((regions, 1, rows, lon), lambda v, me: (0, v + offset, 0, 0)),
                pl.BlockSpec((regions, 1, rows, lon), lambda v, me: (0, variables - 1, 0, 0)),
                pl.BlockSpec((3 * lon, lon), lambda v, me: (0, 0)),
                pl.BlockSpec((every, 3 * every), lambda v, me: (0, 0)),
            ],
            out_specs=block,
            scratch_shapes=[
                pltpu.VMEM((every * members, lon), F32),
                pltpu.VMEM((every // STEP, patches, STEP * lon), BF16),
            ],
        ),
        compiler_params=pltpu.CompilerParams(vmem_limit_bytes=VMEM),
        cost_estimate=pl.CostEstimate(
            flops=count * pairs * patches * 8,
            bytes_accessed=8 * count * every * lon * members,
            transcendentals=0,
        ),
        name="whole_fields",
    )(me, fields, extra, extra, lon_weights(lon), lat_weights(every, 0))


def smooth_kernel(own_ref, low_ref, high_ref, lon_ref, lat_ref, out_ref):
    held = own_ref.shape[0]
    for k in range(held):
        rows = [ref[k, 0] for ref in (low_ref, own_ref, high_ref)]
        wide = along_lon(jnp.concatenate(rows, axis=0), lon_ref[...])
        pad = rows[0].shape[0]
        out_ref[k, 0] = along_lat(wide, lat_ref[...], wide[pad : pad + rows[1].shape[0]])


def smoothed_rows(own):
    held, count, rows, lon = own.shape
    regions = lax.axis_size("region")
    up = [(i, i + 1) for i in range(regions - 1)]
    low = lax.ppermute(own[:, :, rows - HALF :], "region", up)
    high = lax.ppermute(own[:, :, :HALF], "region", [(b, a) for a, b in up])
    edge = pl.BlockSpec((held, 1, HALF, lon), lambda v: (0, v, 0, 0))
    block = pl.BlockSpec((held, 1, rows, lon), lambda v: (0, v, 0, 0))
    span = rows + 2 * HALF
    return pl.pallas_call(
        smooth_kernel,
        out_shape=jax.ShapeDtypeStruct(own.shape, F32),
        grid=(count,),
        in_specs=[
            block,
            edge,
            edge,
            pl.BlockSpec((3 * lon, lon), lambda v: (0, 0)),
            pl.BlockSpec((rows, 3 * span), lambda v: (0, 0)),
        ],
        out_specs=block,
        compiler_params=pltpu.CompilerParams(vmem_limit_bytes=VMEM),
        name="smoothed_rows",
    )(own, low, high, lon_weights(lon), lat_weights(rows, HALF))


def share_kernel(all_ref, own_ref, truth_ref, map_ref, out_ref, cells, hots):
    devices, held, _, rows, lon = all_ref.shape
    members = devices * held
    patches = hots.shape[1]
    scale = float(np.sqrt(PATCH))
    steps = rows // STEP

    @pl.when(pl.program_id(0) == 0)
    def _():
        patch = lax.broadcasted_iota(jnp.int32, (patches, lon), 0).astype(F32)
        for row in range(rows):
            hots[row // STEP, :, row % STEP * lon : (row % STEP + 1) * lon] = (
                patch == map_ref[row : row + 1, :]
            ).astype(BF16)

    for device in range(devices):
        for k in range(held):
            cells[pl.ds(device * held + k, rows, stride=members), :] = all_ref[device, k, 0]

    def gaps(step, j):
        row = step * STEP + j
        a = cells[pl.ds(pl.multiple_of(row * members, members), members), :]
        truth = truth_ref[0, pl.ds(row, 1), :]
        result = []
        for k in range(held):
            own = own_ref[k, 0, pl.ds(row, 1), :]
            result += [own - a, jnp.broadcast_to(own - truth, (8, lon))]
        return row, result

    def first(step, total):
        columns = [
            jnp.concatenate([gap * gap for gap in gaps(step, j)[1]], axis=0) for j in range(STEP)
        ]
        squares = jnp.concatenate(halves(jnp.concatenate(columns, axis=1)), axis=0)
        return total + patch_sums(squares, hots[step])

    height = held * (members + 8)
    total = lax.fori_loop(0, steps, first, jnp.zeros((2 * height, patches), F32))
    weights = lax.rsqrt(total[:height] + total[height:] + EPS)
    place = lax.rem(lax.broadcasted_iota(jnp.int32, (height, patches), 0), members + 8)
    weights = head_and_tail(weights * jnp.where(place < members, -scale / members, scale))

    def second(step, carry):
        spread = on_cells(weights, hots[step])
        for j in range(STEP):
            row, parts = gaps(step, j)
            w = spread[:, j * lon : (j + 1) * lon]
            for k in range(held):
                base = k * (members + 8)
                pull = w[base : base + members] * parts[2 * k]
                toward = w[base + members : base + members + 1] * parts[2 * k + 1][:1]
                out_ref[k, 0, pl.ds(row, 1), :] = toward + jnp.sum(pull, axis=0, keepdims=True)
        return carry

    lax.fori_loop(0, steps, second, 0)


def own_members(everyone, smooth, truth, patch_map):
    held, count, rows, lon = smooth.shape
    devices = everyone.shape[0]
    patches = rows * lon // PATCH
    block = pl.BlockSpec((held, 1, rows, lon), lambda v: (0, v, 0, 0))
    return pl.pallas_call(
        share_kernel,
        out_shape=jax.ShapeDtypeStruct(smooth.shape, F32),
        grid=(count,),
        in_specs=[
            pl.BlockSpec((devices, held, 1, rows, lon), lambda v: (0, 0, v, 0, 0)),
            block,
            pl.BlockSpec((1, rows, lon), lambda v: (v, 0, 0)),
            pl.BlockSpec((rows, lon), lambda v: (0, 0)),
        ],
        out_specs=block,
        scratch_shapes=[
            pltpu.VMEM((rows * devices * held, lon), F32),
            pltpu.VMEM((rows // STEP, patches, STEP * lon), BF16),
        ],
        compiler_params=pltpu.CompilerParams(vmem_limit_bytes=VMEM),
        name="own_members",
    )(everyone, smooth, truth, patch_map)


def patch_of_cell(order, rows, lon):
    position = jnp.arange(rows * lon, dtype=jnp.int32)
    in_row = jnp.arange(rows, dtype=jnp.int32)[:, None] == (order // lon)[None]
    at_lon = (order % lon)[:, None] == jnp.arange(lon, dtype=jnp.int32)[None]
    patch = jnp.where(in_row, (position // PATCH)[None], 0)
    return jnp.dot(
        patch.astype(F32), at_lon.astype(F32), precision=lax.Precision.HIGHEST
    )


def exchange(blocks):
    return lax.all_to_all(blocks, ("region", "member"), 0, 0, tiled=True)


def sent_rows(x, count):
    held, variables, rows, lon = x.shape
    total = variables // count
    x = jnp.transpose(x.reshape(held, total, count, rows, lon), (1, 2, 0, 3, 4))
    return x.reshape(total, count * held * rows, lon)


def kept_rows(blocks, held, rows):
    total, height, lon = blocks.shape
    count = height // (held * rows)
    x = blocks.reshape(total, count, held, rows, lon)
    return jnp.transpose(x, (2, 0, 1, 3, 4)).reshape(held, total * count, rows, lon)


def is_power(n):
    return n & (n - 1) == 0


def sent_pieces(x, regions, devices):
    held, variables, rows, lon = x.shape
    near = devices // variables
    x = x.reshape(held, variables, regions, near, rows // (regions * near), lon)
    x = jnp.transpose(x, (2, 1, 3, 0, 4, 5))
    return x.reshape(regions * devices, -1, lon)


def kept_pieces(blocks, held, variables, regions, devices):
    near = devices // variables
    lon = blocks.shape[-1]
    x = blocks.reshape(regions, variables, near, held, -1, lon)
    return jnp.transpose(x, (3, 1, 0, 2, 4, 5)).reshape(held, variables, -1, lon)


def after(x, first):
    return lax.optimization_barrier((x, first))[0]


def plane_gather(x, near, beside):
    x = x[None]
    first = True
    for axis, size in (("member", near), ("region", lax.axis_size("region"))):
        index, step = lax.axis_index(axis), 1
        while step < size:
            count = lax.axis_size(axis)
            other = lax.ppermute(x, axis, [(i, i ^ step) for i in range(count)])
            if first:
                other, beside = lax.optimization_barrier((other, beside))
                first = False
            low = (index & step) == 0
            x = jnp.concatenate([jnp.where(low, x, other), jnp.where(low, other, x)], axis=0)
            step *= 2
            if axis == "region" and step * 2 == size:
                x, beside = lax.optimization_barrier((x, beside))
    return x, beside


def extras(observed, patch_map, starts, counts):
    regions = lax.axis_size("region")
    region, member = lax.axis_index("region"), lax.axis_index("member")
    result = []
    for shift in range(regions):
        owner = lax.rem(region + shift, regions), member
        pieces = [
            lax.dynamic_slice_in_dim(observed, start(*owner), count, axis=0)
            for start, count in zip(starts, counts)
        ]
        piece = jnp.concatenate(pieces + [patch_map[None]], axis=0)
        if shift:
            ring = [(i, (i + shift) % regions) for i in range(regions)]
            piece = lax.ppermute(piece, "region", ring)
        result.append(piece)
    return jnp.stack(result)


def spread_over_all(forecast, observed, patch_map):
    held, variables, rows, lon = forecast.shape
    regions, devices = lax.axis_size("region"), lax.axis_size("member")
    region, member = lax.axis_index("region"), lax.axis_index("member")
    total = regions * devices
    share = variables // total
    chunks = [count for count in (share - share // 2, share // 2) if count]
    left = variables - share * total
    sent, starts, counts, begin = [], [], [], 0
    for count in chunks:
        sent.append(sent_rows(forecast[:, begin : begin + count * total], count))
        starts.append(lambda r, m, b=begin, c=count: b + (r * devices + m) * c)
        counts.append(count)
        begin += count * total
    if left:
        near = devices // left
        sent[0] = jnp.concatenate(
            [sent[0], sent_pieces(forecast[:, begin:], regions, devices)], axis=1
        )
        starts.append(lambda r, m, b=begin: b + m // near)
        counts.append(1)
    extra = extras(observed, patch_map, starts, counts)
    if len(chunks) > 1:
        sent[1:], extra = lax.optimization_barrier((sent[1:], extra))
    fields = [exchange(part) for part in sent]
    results = [
        whole_fields(field, count, held, extra, sum(chunks[:i]))
        for i, (field, count) in enumerate(zip(fields, chunks))
    ]
    body = chunks[0] * held * rows
    if left:
        piece = rows // (regions * near)
        field, results[0] = plane_gather(fields[0][:, body:], near, results[0])
        field = field.reshape(-1, total, held, piece, lon)
        field = jnp.transpose(field, (1, 2, 0, 3, 4)).reshape(total, held * rows, lon)
        result = whole_fields(field, 1, held, extra, share).reshape(total, held, rows, lon)
        place = region * near + lax.rem(member, near)
        result = lax.dynamic_slice_in_dim(result, place * piece, piece, axis=2)
        results[-1] = jnp.concatenate([results[-1], result.reshape(total, -1, lon)], axis=1)
    backs = []
    for result in results:
        backs.append(exchange(after(result, backs[-1:])))
    parts = [kept_rows(back[:, : count * held * rows], held, rows) for back, count in zip(backs, chunks)]
    if left:
        last = chunks[-1] * held * rows
        parts.append(kept_pieces(backs[-1][:, last:], held, left, regions, devices))
    return jnp.concatenate(parts, axis=1)


def on_device(predicted_states, observed_analysis, tile_location_sequence):
    _, variables, rows, lon = predicted_states.shape
    regions, devices = lax.axis_size("region"), lax.axis_size("member")
    patch_map = patch_of_cell(tile_location_sequence[0], rows, lon)
    left = variables % (regions * devices)
    planes = left == 0 or (
        devices % left == 0
        and rows % (regions * devices // left) == 0
        and is_power(regions)
        and is_power(devices // left)
    )
    if variables >= regions * devices and planes:
        return spread_over_all(predicted_states, observed_analysis, patch_map)
    smooth = smoothed_rows(predicted_states)
    everyone = lax.all_gather(smooth, "member")
    return smoothed_rows(own_members(everyone, smooth, observed_analysis, patch_map))


def solution(mesh):
    in_specs = (P("member", None, "region", None), P(None, "region", None), P("region", None))
    out_specs = P("member", None, "region", None)
    return jax.shard_map(
        on_device, mesh=mesh, in_specs=in_specs, out_specs=out_specs, check_vma=False
    )
```

```python
import functools

import jax
import jax.numpy as jnp
import numpy as np
from jax import lax
from jax.experimental import pallas as pl
from jax.experimental.pallas import tpu as pltpu
from jax.sharding import PartitionSpec as P

HALF = 32
PATCH = 128
EPS = 1e-06
STEP = 32
BLOCK = 8
VMEM = 56 * 1024 * 1024
F32 = jnp.float32
BF16 = jnp.bfloat16


def bell(out_cells, in_cells):
    sigma = HALF / 2.0
    steps = np.arange(-HALF, HALF + 1)
    norm = np.sum(np.exp(-(steps**2) / (2.0 * sigma**2)))
    offset = np.asarray(in_cells)[None, :] - np.asarray(out_cells)[:, None]
    value = 0.5 * np.exp(-(offset**2) / (2.0 * sigma**2)) / norm
    value = jnp.asarray(np.where(np.abs(offset) <= HALF, value, 0.0), F32)
    return halves(value)


def halves(x):
    head = x.astype(BF16)
    return head, (x - head.astype(F32)).astype(BF16)


def lon_weights(lon):
    head, tail = bell(range(lon), range(lon))
    return jnp.block([[head, tail], [head, jnp.zeros_like(tail)]])


def lat_weights(rows, pad):
    head, tail = bell(range(rows), range(-pad, rows + pad))
    return jnp.block([[head, head], [tail, jnp.zeros_like(tail)]])


def along_lon(x, weights):
    lon = x.shape[1]
    both = jnp.concatenate(halves(x), axis=1)
    result = jnp.dot(both, weights, preferred_element_type=F32)
    return 0.5 * x + result[:, :lon] + result[:, lon:]


def along_lat(x, weights, own):
    rows = own.shape[0]
    both = jnp.concatenate(halves(x), axis=0)
    result = jnp.dot(weights, both, preferred_element_type=F32)
    return 0.5 * own + result[:rows] + result[rows:]


def patch_sums(squares, hot):
    return lax.dot_general(
        squares,
        hot,
        (((1,), (1,)), ((), ())),
        preferred_element_type=F32,
    )


def on_cells(weights, hot):
    return jnp.dot(weights, jnp.concatenate([hot, hot], axis=0), preferred_element_type=F32)


def head_and_tail(weights):
    return jnp.concatenate(halves(weights), axis=1)


def member_gaps(blocks):
    gaps = [x - pltpu.roll(x, s, 0) for x in blocks for s in range(1, BLOCK // 2 + 1)]
    for b, x in enumerate(blocks):
        for y in blocks[b + 1 :]:
            gaps.append(x - y)
            gaps += [x - pltpu.roll(y, s, 0) for s in range(1, BLOCK)]
    return gaps


def member_pulls(pulls, count):
    pulls = iter(pulls)
    sums = [0.0] * count
    for b in range(count):
        for s in range(1, BLOCK // 2 + 1):
            pull = next(pulls)
            sums[b] = sums[b] + pull
            if 2 * s != BLOCK:
                sums[b] = sums[b] - pltpu.roll(pull, BLOCK - s, 0)
    for b in range(count):
        for c in range(b + 1, count):
            for s in range(BLOCK):
                pull = next(pulls)
                sums[b] = sums[b] + pull
                sums[c] = sums[c] - (pltpu.roll(pull, BLOCK - s, 0) if s else pull)
    return sums


def field_kernel(
    regions, places_ref, field_ref, truth_ref, hots, lon_ref, lat_ref, out_ref, cells
):
    outer, _, inner, _, lon = field_ref.shape
    rows = truth_ref.shape[2]
    held = field_ref.shape[3] // rows
    devices = outer * inner // regions
    members = devices * held
    blocks = members // BLOCK
    pairs = blocks * (BLOCK // 2) + blocks * (blocks - 1) // 2 * BLOCK
    height = (pairs + blocks) * BLOCK
    steps = rows // STEP
    patches = hots.shape[1]
    scale = float(np.sqrt(PATCH))

    def shift_of(region):
        return lax.rem(places_ref[0] - region + regions, regions)

    def place(region, device):
        index = places_ref[1 + region * devices + device]
        return (index, 0, 0) if inner == 1 else (index // inner, 0, index % inner)

    def smoothed(pair):
        wide = jnp.concatenate([along_lon(x, lon_ref[...]) for x in pair], axis=1)
        return along_lat(wide, lat_ref[...], wide)

    every = regions * rows
    for device in range(devices):
        pair = [
            jnp.concatenate(
                [
                    field_ref[*place(region, device), k * rows : (k + 1) * rows, :]
                    for region in range(regions)
                ],
                axis=0,
            )
            for k in range(held)
        ]
        result = smoothed(pair)
        for k in range(held):
            cells[pl.ds(device * held + k, every, stride=members), :] = result[
                :, k * lon : (k + 1) * lon
            ]

    for region in range(regions):
        shift = shift_of(region)

        def load(row):
            start = pl.multiple_of((region * rows + row) * members, members)
            a = [cells[pl.ds(start + b * BLOCK, BLOCK), :] for b in range(blocks)]
            truth = truth_ref[shift, 0, pl.ds(row, 1), :]
            return start, member_gaps(a) + [x - truth for x in a]

        def first(step, total):
            heads, tails = [], []
            for j in range(STEP):
                head, tail = halves(
                    jnp.concatenate([gap * gap for gap in load(step * STEP + j)[1]], axis=0)
                )
                heads.append(head)
                tails.append(tail)
            squares = jnp.concatenate(
                [jnp.concatenate(heads, axis=1), jnp.concatenate(tails, axis=1)], axis=0
            )
            return total + patch_sums(squares, hots[region * steps + step])

        total = lax.fori_loop(0, steps, first, jnp.zeros((2 * height, patches), F32))
        weights = lax.rsqrt(total[:height] + total[height:] + EPS)
        factor = jnp.where(
            lax.broadcasted_iota(jnp.int32, (height, patches), 0) < pairs * BLOCK,
            -scale / members,
            scale,
        )
        weights = head_and_tail(weights * factor)

        def second(step, carry):
            spread = on_cells(weights, hots[region * steps + step])
            for j in range(STEP):
                start, gaps = load(step * STEP + j)
                w = spread[:, j * lon : (j + 1) * lon]
                terms = [w[i * BLOCK : (i + 1) * BLOCK] * gap for i, gap in enumerate(gaps)]
                sums = member_pulls(terms[:pairs], blocks)
                for b in range(blocks):
                    cells[pl.ds(start + b * BLOCK, BLOCK), :] = sums[b] + terms[pairs + b]
            return carry

        lax.fori_loop(0, steps, second, 0)

    for device in range(devices):
        result = smoothed(
            [cells[pl.ds(device * held + k, every, stride=members), :] for k in range(held)]
        )
        for region in range(regions):
            for k in range(held):
                out_ref[*place(region, device), k * rows : (k + 1) * rows, :] = result[
                    region * rows : (region + 1) * rows, k * lon : (k + 1) * lon
                ]


def hots_kernel(region_ref, extra_ref, hots):
    regions, _, rows, lon = extra_ref.shape
    _, patches, _ = hots.shape
    steps = rows // STEP
    patch = lax.broadcasted_iota(jnp.int32, (patches, lon), 0).astype(F32)
    for region in range(regions):
        shift = lax.rem(region_ref[0] - region + regions, regions)
        for row in range(rows):
            block, j = region * steps + row // STEP, row % STEP
            own = extra_ref[shift, 0, row : row + 1, :]
            hots[block, :, j * lon : (j + 1) * lon] = (patch == own).astype(BF16)


def patch_hots(extra):
    regions, variables, rows, lon = extra.shape
    shape = (regions * rows // STEP, rows * lon // PATCH, STEP * lon)
    return pl.pallas_call(
        hots_kernel,
        out_shape=jax.ShapeDtypeStruct(shape, BF16),
        grid=(1,),
        in_specs=[
            pl.BlockSpec(memory_space=pltpu.SMEM),
            pl.BlockSpec((regions, 1, rows, lon), lambda i: (0, variables - 1, 0, 0)),
        ],
        out_specs=pl.BlockSpec(shape, lambda i: (0, 0, 0)),
        compiler_params=pltpu.CompilerParams(vmem_limit_bytes=VMEM),
        name="patch_hots",
    )(lax.axis_index("region").reshape(1), extra)


def whole_fields(fields, places, extra, hots, offset):
    outer, count, inner, height, lon = fields.shape
    regions, variables, rows, _ = extra.shape
    members = outer * inner // regions * (height // rows)
    patches = rows * lon // PATCH
    every = regions * rows
    table = jnp.concatenate([lax.axis_index("region").reshape(1), places])
    block = pl.BlockSpec((outer, 1, inner, height, lon), lambda v, table: (0, v, 0, 0, 0))
    pairs = every * lon * members * (members // 2 + 1)
    return pl.pallas_call(
        functools.partial(field_kernel, regions),
        out_shape=jax.ShapeDtypeStruct(fields.shape, F32),
        grid_spec=pltpu.PrefetchScalarGridSpec(
            num_scalar_prefetch=1,
            grid=(count,),
            in_specs=[
                block,
                pl.BlockSpec((regions, 1, rows, lon), lambda v, table: (0, v + offset, 0, 0)),
                pl.BlockSpec(hots.shape, lambda v, table: (0, 0, 0)),
                pl.BlockSpec((2 * lon, 2 * lon), lambda v, table: (0, 0)),
                pl.BlockSpec((2 * every, 2 * every), lambda v, table: (0, 0)),
            ],
            out_specs=block,
            scratch_shapes=[
                pltpu.VMEM((every * members, lon), F32),
            ],
        ),
        compiler_params=pltpu.CompilerParams(vmem_limit_bytes=VMEM),
        cost_estimate=pl.CostEstimate(
            flops=count * pairs * patches * 8, bytes_accessed=8 * fields.size, transcendentals=0
        ),
        name="whole_fields",
    )(table, fields, extra, hots, lon_weights(lon), lat_weights(every, 0))


def smooth_kernel(own_ref, low_ref, high_ref, lon_ref, lat_ref, out_ref):
    held = own_ref.shape[0]
    for k in range(held):
        rows = [ref[k, 0] for ref in (low_ref, own_ref, high_ref)]
        wide = along_lon(jnp.concatenate(rows, axis=0), lon_ref[...])
        pad = rows[0].shape[0]
        out_ref[k, 0] = along_lat(wide, lat_ref[...], wide[pad : pad + rows[1].shape[0]])


def smoothed_rows(own):
    held, count, rows, lon = own.shape
    regions = lax.axis_size("region")
    up = [(i, i + 1) for i in range(regions - 1)]
    low = lax.ppermute(own[:, :, rows - HALF :], "region", up)
    high = lax.ppermute(own[:, :, :HALF], "region", [(b, a) for a, b in up])
    edge = pl.BlockSpec((held, 1, HALF, lon), lambda v: (0, v, 0, 0))
    block = pl.BlockSpec((held, 1, rows, lon), lambda v: (0, v, 0, 0))
    span = rows + 2 * HALF
    return pl.pallas_call(
        smooth_kernel,
        out_shape=jax.ShapeDtypeStruct(own.shape, F32),
        grid=(count,),
        in_specs=[
            block,
            edge,
            edge,
            pl.BlockSpec((2 * lon, 2 * lon), lambda v: (0, 0)),
            pl.BlockSpec((2 * rows, 2 * span), lambda v: (0, 0)),
        ],
        out_specs=block,
        compiler_params=pltpu.CompilerParams(vmem_limit_bytes=VMEM),
        name="smoothed_rows",
    )(own, low, high, lon_weights(lon), lat_weights(rows, HALF))


def share_kernel(all_ref, own_ref, truth_ref, map_ref, out_ref, cells, hots):
    devices, held, _, rows, lon = all_ref.shape
    members = devices * held
    patches = hots.shape[1]
    scale = float(np.sqrt(PATCH))
    steps = rows // STEP

    @pl.when(pl.program_id(0) == 0)
    def _():
        patch = lax.broadcasted_iota(jnp.int32, (patches, lon), 0).astype(F32)
        for row in range(rows):
            hots[row // STEP, :, row % STEP * lon : (row % STEP + 1) * lon] = (
                patch == map_ref[row : row + 1, :]
            ).astype(BF16)

    for device in range(devices):
        for k in range(held):
            cells[pl.ds(device * held + k, rows, stride=members), :] = all_ref[device, k, 0]

    def gaps(step, j):
        row = step * STEP + j
        a = cells[pl.ds(pl.multiple_of(row * members, members), members), :]
        truth = truth_ref[0, pl.ds(row, 1), :]
        result = []
        for k in range(held):
            own = own_ref[k, 0, pl.ds(row, 1), :]
            result += [own - a, jnp.broadcast_to(own - truth, (8, lon))]
        return row, result

    def first(step, total):
        columns = [
            jnp.concatenate([gap * gap for gap in gaps(step, j)[1]], axis=0) for j in range(STEP)
        ]
        squares = jnp.concatenate(halves(jnp.concatenate(columns, axis=1)), axis=0)
        return total + patch_sums(squares, hots[step])

    height = held * (members + 8)
    total = lax.fori_loop(0, steps, first, jnp.zeros((2 * height, patches), F32))
    weights = lax.rsqrt(total[:height] + total[height:] + EPS)
    place = lax.rem(lax.broadcasted_iota(jnp.int32, (height, patches), 0), members + 8)
    weights = head_and_tail(weights * jnp.where(place < members, -scale / members, scale))

    def second(step, carry):
        spread = on_cells(weights, hots[step])
        for j in range(STEP):
            row, parts = gaps(step, j)
            w = spread[:, j * lon : (j + 1) * lon]
            for k in range(held):
                base = k * (members + 8)
                pull = w[base : base + members] * parts[2 * k]
                toward = w[base + members : base + members + 1] * parts[2 * k + 1][:1]
                out_ref[k, 0, pl.ds(row, 1), :] = toward + jnp.sum(pull, axis=0, keepdims=True)
        return carry

    lax.fori_loop(0, steps, second, 0)


def own_members(everyone, smooth, truth, patch_map):
    held, count, rows, lon = smooth.shape
    devices = everyone.shape[0]
    patches = rows * lon // PATCH
    block = pl.BlockSpec((held, 1, rows, lon), lambda v: (0, v, 0, 0))
    return pl.pallas_call(
        share_kernel,
        out_shape=jax.ShapeDtypeStruct(smooth.shape, F32),
        grid=(count,),
        in_specs=[
            pl.BlockSpec((devices, held, 1, rows, lon), lambda v: (0, 0, v, 0, 0)),
            block,
            pl.BlockSpec((1, rows, lon), lambda v: (v, 0, 0)),
            pl.BlockSpec((rows, lon), lambda v: (0, 0)),
        ],
        out_specs=block,
        scratch_shapes=[
            pltpu.VMEM((rows * devices * held, lon), F32),
            pltpu.VMEM((rows // STEP, patches, STEP * lon), BF16),
        ],
        compiler_params=pltpu.CompilerParams(vmem_limit_bytes=VMEM),
        name="own_members",
    )(everyone, smooth, truth, patch_map)


def patch_of_cell(order, rows, lon):
    position = jnp.arange(rows * lon, dtype=jnp.int32)
    in_row = jnp.arange(rows, dtype=jnp.int32)[:, None] == (order // lon)[None]
    at_lon = (order % lon)[:, None] == jnp.arange(lon, dtype=jnp.int32)[None]
    patch = jnp.where(in_row, (position // PATCH)[None], 0)
    return jnp.dot(
        patch.astype(F32), at_lon.astype(F32), precision=lax.Precision.HIGHEST
    )


def exchange(blocks):
    return lax.all_to_all(blocks, ("region", "member"), 0, 0, tiled=True)


def sent_rows(x, count):
    held, variables, rows, lon = x.shape
    total = variables // count
    x = jnp.transpose(x.reshape(held, total, count, rows, lon), (1, 2, 0, 3, 4))
    return x.reshape(total, count, 1, held * rows, lon)


def kept_rows(blocks, rows):
    total, count, _, height, lon = blocks.shape
    x = blocks.reshape(total, count, height // rows, rows, lon)
    return jnp.transpose(x, (2, 0, 1, 3, 4)).reshape(height // rows, total * count, rows, lon)


def is_power(n):
    return n & (n - 1) == 0


def shifted(x, places):
    count = lax.axis_size("member")
    return lax.ppermute(x, "member", [(i, (i + places) % count) for i in range(count)])


def plane_steps(near):
    regions = lax.axis_size("region")
    far = [("region", 1 << bit) for bit in range(1, regions.bit_length() - 1)][::-1]
    beside = [("member", 1 << bit) for bit in range(near.bit_length() - 1)]
    return far + beside + [("region", 1)] * (regions > 1)


def plane_gather(x, near, beside):
    x = x[None]
    steps = plane_steps(near)
    for i, (axis, step) in enumerate(steps):
        count = lax.axis_size(axis)
        other = lax.ppermute(x, axis, [(j, j ^ step) for j in range(count)])
        if i == 0:
            other, beside = lax.optimization_barrier((other, beside))
        x = jnp.concatenate([x, other], axis=0)
        if i == len(steps) - 2:
            x, beside = lax.optimization_barrier((x, beside))
    return x, beside


def plane_index(region, member, near):
    steps, index = plane_steps(near), 0
    for i, (axis, step) in enumerate(steps):
        other = region if axis == "region" else member % near
        own = lax.axis_index(axis) if axis == "region" else lax.axis_index(axis) % near
        index = index + jnp.where((other ^ own) & step, 1 << i, 0)
    return index


def extras(observed, patch_map, starts, counts):
    regions = lax.axis_size("region")
    region, member = lax.axis_index("region"), lax.axis_index("member")
    result = []
    for shift in range(regions):
        owner = lax.rem(region + shift, regions), member
        pieces = [
            lax.dynamic_slice_in_dim(observed, start(*owner), count, axis=0)
            for start, count in zip(starts, counts)
        ]
        piece = jnp.concatenate(pieces + [patch_map[None]], axis=0)
        if shift:
            ring = [(i, (i + shift) % regions) for i in range(regions)]
            piece = lax.ppermute(piece, "region", ring)
        result.append(piece)
    return jnp.stack(result)


def spread_over_all(forecast, observed, patch_map):
    held, variables, rows, lon = forecast.shape
    regions, devices = lax.axis_size("region"), lax.axis_size("member")
    region, member = lax.axis_index("region"), lax.axis_index("member")
    total = regions * devices
    share = variables // total
    whole = share * total
    left = variables - whole
    chunks = [count for count in (share - share // 2, share // 2) if count]
    sent, starts, counts, begin = [], [], [], 0
    for count in chunks:
        sent.append(sent_rows(forecast[:, begin : begin + count * total], count))
        starts.append(lambda r, m, b=begin, c=count: b + (r * devices + m) * c)
        counts.append(count)
        begin += count * total
    shifts = []
    if left:
        near = devices // left
        plane = member // near
        starts.append(lambda r, m, b=begin: b + m // near)
        counts.append(1)
        for t in range(left):
            first = begin + lax.rem(plane + t, left)
            x = lax.dynamic_slice_in_dim(forecast, first, 1, axis=1).reshape(held * rows, lon)
            shifts.append(shifted(x, t * near) if t else x)
    extra = extras(observed, patch_map, starts, counts)
    hots = patch_hots(extra)
    if len(chunks) > 1:
        sent[1:], extra, hots, shifts = lax.optimization_barrier((sent[1:], extra, hots, shifts))
    order = jnp.arange(total, dtype=jnp.int32)
    results = [
        whole_fields(exchange(part), order, extra, hots, sum(chunks[:i])) for i, part in enumerate(sent)
    ]
    if left:
        field, results[0] = plane_gather(jnp.stack(shifts), near, results[0])
        members = order % devices
        places = plane_index(order // devices, members, near) * left
        places = places + (plane - members // near) % left
        result = whole_fields(field[:, None], places, extra, hots, share)
        result = result[0, 0]
        shifts = [shifted(result[t], -t * near) if t else result[t] for t in range(left)]
        shifts = jnp.stack(shifts + shifts).reshape(2 * left, held, rows, lon)
        last = lax.dynamic_slice_in_dim(shifts, lax.rem(left - plane, left), left, axis=0)
        last = jnp.swapaxes(last, 0, 1)
        if len(chunks) > 1:
            results[1], last = lax.optimization_barrier((results[1], last))
    backs = []
    for result in results:
        if backs:
            result, backs[-1] = lax.optimization_barrier((result, backs[-1]))
        backs.append(exchange(result))
    parts = [kept_rows(back, rows) for back in backs]
    if left:
        parts.insert(1, last)
    out = jnp.concatenate(
        parts[:1] + [jnp.zeros((held, variables - parts[0].shape[1], rows, lon), F32)], axis=1
    )
    places = [parts[0].shape[1]] * 2
    if left:
        places = [whole, parts[0].shape[1]]
    for part, first in zip(parts[1:], places):
        out = lax.dynamic_update_slice_in_dim(out, part, first, axis=1)
    return out


def on_device(predicted_states, observed_analysis, tile_location_sequence):
    _, variables, rows, lon = predicted_states.shape
    regions, devices = lax.axis_size("region"), lax.axis_size("member")
    patch_map = patch_of_cell(tile_location_sequence[0], rows, lon)
    left = variables % (regions * devices)
    planes = left == 0 or (
        devices % left == 0 and is_power(regions) and is_power(devices // left)
    )
    if variables >= regions * devices and planes:
        return spread_over_all(predicted_states, observed_analysis, patch_map)
    smooth = smoothed_rows(predicted_states)
    everyone = lax.all_gather(smooth, "member")
    return smoothed_rows(own_members(everyone, smooth, observed_analysis, patch_map))


def solution(mesh):
    in_specs = (P("member", None, "region", None), P(None, "region", None), P("region", None))
    out_specs = P("member", None, "region", None)
    return jax.shard_map(
        on_device, mesh=mesh, in_specs=in_specs, out_specs=out_specs, check_vma=False
    )
```

```python
import functools

import jax
import jax.numpy as jnp
import numpy as np
from jax import lax
from jax.experimental import pallas as pl
from jax.experimental.pallas import tpu as pltpu
from jax.sharding import PartitionSpec as P

HALF = 32
PATCH = 128
EPS = 1e-06
STEP = 32
BLOCK = 8
VMEM = 56 * 1024 * 1024
F32 = jnp.float32
BF16 = jnp.bfloat16


def bell(out_cells, in_cells):
    sigma = HALF / 2.0
    steps = np.arange(-HALF, HALF + 1)
    norm = np.sum(np.exp(-(steps**2) / (2.0 * sigma**2)))
    offset = np.asarray(in_cells)[None, :] - np.asarray(out_cells)[:, None]
    value = 0.5 * np.exp(-(offset**2) / (2.0 * sigma**2)) / norm
    value = jnp.asarray(np.where(np.abs(offset) <= HALF, value, 0.0), F32)
    return halves(value)


def halves(x):
    head = x.astype(BF16)
    return head, (x - head.astype(F32)).astype(BF16)


def lon_weights(lon):
    head, tail = bell(range(lon), range(lon))
    return jnp.block([[head, tail], [head, jnp.zeros_like(tail)]])


def lat_weights(rows, pad):
    head, tail = bell(range(rows), range(-pad, rows + pad))
    return jnp.block([[head, head], [tail, jnp.zeros_like(tail)]])


def along_lon(x, weights):
    lon = x.shape[1]
    both = jnp.concatenate(halves(x), axis=1)
    result = jnp.dot(both, weights, preferred_element_type=F32)
    return 0.5 * x + result[:, :lon] + result[:, lon:]


def along_lat(x, weights, own):
    rows = own.shape[0]
    both = jnp.concatenate(halves(x), axis=0)
    result = jnp.dot(weights, both, preferred_element_type=F32)
    return 0.5 * own + result[:rows] + result[rows:]


def patch_sums(squares, hot):
    return lax.dot_general(
        squares,
        hot,
        (((1,), (1,)), ((), ())),
        preferred_element_type=F32,
    )


def on_cells(weights, hot):
    return jnp.dot(weights, jnp.concatenate([hot, hot], axis=0), preferred_element_type=F32)


def head_and_tail(weights):
    return jnp.concatenate(halves(weights), axis=1)


def member_gaps(blocks):
    gaps = [x - pltpu.roll(x, s, 0) for x in blocks for s in range(1, BLOCK // 2 + 1)]
    for b, x in enumerate(blocks):
        for y in blocks[b + 1 :]:
            gaps.append(x - y)
            gaps += [x - pltpu.roll(y, s, 0) for s in range(1, BLOCK)]
    return gaps


def member_pulls(pulls, count):
    pulls = iter(pulls)
    sums = [0.0] * count
    for b in range(count):
        for s in range(1, BLOCK // 2 + 1):
            pull = next(pulls)
            sums[b] = sums[b] + pull
            if 2 * s != BLOCK:
                sums[b] = sums[b] - pltpu.roll(pull, BLOCK - s, 0)
    for b in range(count):
        for c in range(b + 1, count):
            for s in range(BLOCK):
                pull = next(pulls)
                sums[b] = sums[b] + pull
                sums[c] = sums[c] - (pltpu.roll(pull, BLOCK - s, 0) if s else pull)
    return sums


def field_kernel(
    regions, places_ref, field_ref, truth_ref, hots, lon_ref, lat_ref, out_ref, cells
):
    outer, _, inner, _, lon = field_ref.shape
    rows = truth_ref.shape[2]
    held = field_ref.shape[3] // rows
    devices = outer * inner // regions
    members = devices * held
    blocks = members // BLOCK
    pairs = blocks * (BLOCK // 2) + blocks * (blocks - 1) // 2 * BLOCK
    height = (pairs + blocks) * BLOCK
    steps = rows // STEP
    patches = hots.shape[1]
    scale = float(np.sqrt(PATCH))

    def shift_of(region):
        return lax.rem(places_ref[0] - region + regions, regions)

    def place(region, device):
        index = places_ref[1 + region * devices + device]
        return (index, 0, 0) if inner == 1 else (index // inner, 0, index % inner)

    def smoothed(pair):
        wide = jnp.concatenate([along_lon(x, lon_ref[...]) for x in pair], axis=1)
        return along_lat(wide, lat_ref[...], wide)

    every = regions * rows
    for device in range(devices):
        pair = [
            jnp.concatenate(
                [
                    field_ref[*place(region, device), k * rows : (k + 1) * rows, :]
                    for region in range(regions)
                ],
                axis=0,
            )
            for k in range(held)
        ]
        result = smoothed(pair)
        for k in range(held):
            cells[pl.ds(device * held + k, every, stride=members), :] = result[
                :, k * lon : (k + 1) * lon
            ]

    for region in range(regions):
        shift = shift_of(region)

        def load(row):
            start = pl.multiple_of((region * rows + row) * members, members)
            a = [cells[pl.ds(start + b * BLOCK, BLOCK), :] for b in range(blocks)]
            truth = truth_ref[shift, 0, pl.ds(row, 1), :]
            return start, member_gaps(a) + [x - truth for x in a]

        def first(step, total):
            heads, tails = [], []
            for j in range(STEP):
                head, tail = halves(
                    jnp.concatenate([gap * gap for gap in load(step * STEP + j)[1]], axis=0)
                )
                heads.append(head)
                tails.append(tail)
            squares = jnp.concatenate(
                [jnp.concatenate(heads, axis=1), jnp.concatenate(tails, axis=1)], axis=0
            )
            return total + patch_sums(squares, hots[region * steps + step])

        total = lax.fori_loop(0, steps, first, jnp.zeros((2 * height, patches), F32))
        weights = lax.rsqrt(total[:height] + total[height:] + EPS)
        factor = jnp.where(
            lax.broadcasted_iota(jnp.int32, (height, patches), 0) < pairs * BLOCK,
            -scale / members,
            scale,
        )
        weights = head_and_tail(weights * factor)

        def second(step, carry):
            spread = on_cells(weights, hots[region * steps + step])
            for j in range(STEP):
                start, gaps = load(step * STEP + j)
                w = spread[:, j * lon : (j + 1) * lon]
                terms = [w[i * BLOCK : (i + 1) * BLOCK] * gap for i, gap in enumerate(gaps)]
                sums = member_pulls(terms[:pairs], blocks)
                for b in range(blocks):
                    cells[pl.ds(start + b * BLOCK, BLOCK), :] = sums[b] + terms[pairs + b]
            return carry

        lax.fori_loop(0, steps, second, 0)

    for device in range(devices):
        result = smoothed(
            [cells[pl.ds(device * held + k, every, stride=members), :] for k in range(held)]
        )
        for region in range(regions):
            for k in range(held):
                out_ref[*place(region, device), k * rows : (k + 1) * rows, :] = result[
                    region * rows : (region + 1) * rows, k * lon : (k + 1) * lon
                ]


def hots_kernel(region_ref, extra_ref, hots):
    regions, _, rows, lon = extra_ref.shape
    _, patches, _ = hots.shape
    steps = rows // STEP
    patch = lax.broadcasted_iota(jnp.int32, (patches, lon), 0).astype(F32)
    for region in range(regions):
        shift = lax.rem(region_ref[0] - region + regions, regions)
        for row in range(rows):
            block, j = region * steps + row // STEP, row % STEP
            own = extra_ref[shift, 0, row : row + 1, :]
            hots[block, :, j * lon : (j + 1) * lon] = (patch == own).astype(BF16)


def patch_hots(extra):
    regions, variables, rows, lon = extra.shape
    shape = (regions * rows // STEP, rows * lon // PATCH, STEP * lon)
    return pl.pallas_call(
        hots_kernel,
        out_shape=jax.ShapeDtypeStruct(shape, BF16),
        grid=(1,),
        in_specs=[
            pl.BlockSpec(memory_space=pltpu.SMEM),
            pl.BlockSpec((regions, 1, rows, lon), lambda i: (0, variables - 1, 0, 0)),
        ],
        out_specs=pl.BlockSpec(shape, lambda i: (0, 0, 0)),
        compiler_params=pltpu.CompilerParams(vmem_limit_bytes=VMEM),
        name="patch_hots",
    )(lax.axis_index("region").reshape(1), extra)


def whole_fields(fields, places, extra, hots, offset):
    outer, count, inner, height, lon = fields.shape
    regions, variables, rows, _ = extra.shape
    members = outer * inner // regions * (height // rows)
    patches = rows * lon // PATCH
    every = regions * rows
    table = jnp.concatenate([lax.axis_index("region").reshape(1), places])
    block = pl.BlockSpec((outer, 1, inner, height, lon), lambda v, table: (0, v, 0, 0, 0))
    pairs = every * lon * members * (members // 2 + 1)
    return pl.pallas_call(
        functools.partial(field_kernel, regions),
        out_shape=jax.ShapeDtypeStruct(fields.shape, F32),
        grid_spec=pltpu.PrefetchScalarGridSpec(
            num_scalar_prefetch=1,
            grid=(count,),
            in_specs=[
                block,
                pl.BlockSpec((regions, 1, rows, lon), lambda v, table: (0, v + offset, 0, 0)),
                pl.BlockSpec(hots.shape, lambda v, table: (0, 0, 0)),
                pl.BlockSpec((2 * lon, 2 * lon), lambda v, table: (0, 0)),
                pl.BlockSpec((2 * every, 2 * every), lambda v, table: (0, 0)),
            ],
            out_specs=block,
            scratch_shapes=[
                pltpu.VMEM((every * members, lon), F32),
            ],
        ),
        compiler_params=pltpu.CompilerParams(vmem_limit_bytes=VMEM),
        cost_estimate=pl.CostEstimate(
            flops=count * pairs * patches * 8, bytes_accessed=8 * fields.size, transcendentals=0
        ),
        name="whole_fields",
    )(table, fields, extra, hots, lon_weights(lon), lat_weights(every, 0))


def smooth_kernel(own_ref, low_ref, high_ref, lon_ref, lat_ref, out_ref):
    held = own_ref.shape[0]
    for k in range(held):
        rows = [ref[k, 0] for ref in (low_ref, own_ref, high_ref)]
        wide = along_lon(jnp.concatenate(rows, axis=0), lon_ref[...])
        pad = rows[0].shape[0]
        out_ref[k, 0] = along_lat(wide, lat_ref[...], wide[pad : pad + rows[1].shape[0]])


def smoothed_rows(own):
    held, count, rows, lon = own.shape
    regions = lax.axis_size("region")
    up = [(i, i + 1) for i in range(regions - 1)]
    low = lax.ppermute(own[:, :, rows - HALF :], "region", up)
    high = lax.ppermute(own[:, :, :HALF], "region", [(b, a) for a, b in up])
    edge = pl.BlockSpec((held, 1, HALF, lon), lambda v: (0, v, 0, 0))
    block = pl.BlockSpec((held, 1, rows, lon), lambda v: (0, v, 0, 0))
    span = rows + 2 * HALF
    return pl.pallas_call(
        smooth_kernel,
        out_shape=jax.ShapeDtypeStruct(own.shape, F32),
        grid=(count,),
        in_specs=[
            block,
            edge,
            edge,
            pl.BlockSpec((2 * lon, 2 * lon), lambda v: (0, 0)),
            pl.BlockSpec((2 * rows, 2 * span), lambda v: (0, 0)),
        ],
        out_specs=block,
        compiler_params=pltpu.CompilerParams(vmem_limit_bytes=VMEM),
        name="smoothed_rows",
    )(own, low, high, lon_weights(lon), lat_weights(rows, HALF))


def share_kernel(all_ref, own_ref, truth_ref, map_ref, out_ref, cells, hots):
    devices, held, _, rows, lon = all_ref.shape
    members = devices * held
    patches = hots.shape[1]
    scale = float(np.sqrt(PATCH))
    steps = rows // STEP

    @pl.when(pl.program_id(0) == 0)
    def _():
        patch = lax.broadcasted_iota(jnp.int32, (patches, lon), 0).astype(F32)
        for row in range(rows):
            hots[row // STEP, :, row % STEP * lon : (row % STEP + 1) * lon] = (
                patch == map_ref[row : row + 1, :]
            ).astype(BF16)

    for device in range(devices):
        for k in range(held):
            cells[pl.ds(device * held + k, rows, stride=members), :] = all_ref[device, k, 0]

    def gaps(step, j):
        row = step * STEP + j
        a = cells[pl.ds(pl.multiple_of(row * members, members), members), :]
        truth = truth_ref[0, pl.ds(row, 1), :]
        result = []
        for k in range(held):
            own = own_ref[k, 0, pl.ds(row, 1), :]
            result += [own - a, jnp.broadcast_to(own - truth, (8, lon))]
        return row, result

    def first(step, total):
        columns = [
            jnp.concatenate([gap * gap for gap in gaps(step, j)[1]], axis=0) for j in range(STEP)
        ]
        squares = jnp.concatenate(halves(jnp.concatenate(columns, axis=1)), axis=0)
        return total + patch_sums(squares, hots[step])

    height = held * (members + 8)
    total = lax.fori_loop(0, steps, first, jnp.zeros((2 * height, patches), F32))
    weights = lax.rsqrt(total[:height] + total[height:] + EPS)
    place = lax.rem(lax.broadcasted_iota(jnp.int32, (height, patches), 0), members + 8)
    weights = head_and_tail(weights * jnp.where(place < members, -scale / members, scale))

    def second(step, carry):
        spread = on_cells(weights, hots[step])
        for j in range(STEP):
            row, parts = gaps(step, j)
            w = spread[:, j * lon : (j + 1) * lon]
            for k in range(held):
                base = k * (members + 8)
                pull = w[base : base + members] * parts[2 * k]
                toward = w[base + members : base + members + 1] * parts[2 * k + 1][:1]
                out_ref[k, 0, pl.ds(row, 1), :] = toward + jnp.sum(pull, axis=0, keepdims=True)
        return carry

    lax.fori_loop(0, steps, second, 0)


def own_members(everyone, smooth, truth, patch_map):
    held, count, rows, lon = smooth.shape
    devices = everyone.shape[0]
    patches = rows * lon // PATCH
    block = pl.BlockSpec((held, 1, rows, lon), lambda v: (0, v, 0, 0))
    return pl.pallas_call(
        share_kernel,
        out_shape=jax.ShapeDtypeStruct(smooth.shape, F32),
        grid=(count,),
        in_specs=[
            pl.BlockSpec((devices, held, 1, rows, lon), lambda v: (0, 0, v, 0, 0)),
            block,
            pl.BlockSpec((1, rows, lon), lambda v: (v, 0, 0)),
            pl.BlockSpec((rows, lon), lambda v: (0, 0)),
        ],
        out_specs=block,
        scratch_shapes=[
            pltpu.VMEM((rows * devices * held, lon), F32),
            pltpu.VMEM((rows // STEP, patches, STEP * lon), BF16),
        ],
        compiler_params=pltpu.CompilerParams(vmem_limit_bytes=VMEM),
        name="own_members",
    )(everyone, smooth, truth, patch_map)


def patch_of_cell(order, rows, lon):
    position = jnp.arange(rows * lon, dtype=jnp.int32)
    in_row = jnp.arange(rows, dtype=jnp.int32)[:, None] == (order // lon)[None]
    at_lon = (order % lon)[:, None] == jnp.arange(lon, dtype=jnp.int32)[None]
    patch = jnp.where(in_row, (position // PATCH)[None], 0)
    return jnp.dot(
        patch.astype(F32), at_lon.astype(F32), precision=lax.Precision.HIGHEST
    )


def exchange(blocks):
    return lax.all_to_all(blocks, ("region", "member"), 0, 0, tiled=True)


def sent_rows(x, count):
    held, variables, rows, lon = x.shape
    total = variables // count
    x = jnp.transpose(x.reshape(held, total, count, rows, lon), (1, 2, 0, 3, 4))
    return x.reshape(total, count, 1, held * rows, lon)


def kept_rows(blocks, rows):
    total, count, _, height, lon = blocks.shape
    x = blocks.reshape(total, count, height // rows, rows, lon)
    return jnp.transpose(x, (2, 0, 1, 3, 4)).reshape(height // rows, total * count, rows, lon)


def is_power(n):
    return n & (n - 1) == 0


def shifted(x, places):
    count = lax.axis_size("member")
    return lax.ppermute(x, "member", [(i, (i + places) % count) for i in range(count)])


def plane_steps(near):
    regions = lax.axis_size("region")
    far = [("region", 1 << bit) for bit in range(1, regions.bit_length() - 1)][::-1]
    beside = [("member", 1 << bit) for bit in range(near.bit_length() - 1)]
    return far + beside + [("region", 1)] * (regions > 1)


def plane_gather(x, near, beside):
    beside = list(beside)
    x = x[None]
    steps = plane_steps(near)
    for i, (axis, step) in enumerate(steps):
        count = lax.axis_size(axis)
        other = lax.ppermute(x, axis, [(j, j ^ step) for j in range(count)])
        if i < len(beside):
            other, beside[i] = lax.optimization_barrier((other, beside[i]))
        x = jnp.concatenate([x, other], axis=0)
    return x, beside


def plane_index(region, member, near):
    steps, index = plane_steps(near), 0
    for i, (axis, step) in enumerate(steps):
        other = region if axis == "region" else member % near
        own = lax.axis_index(axis) if axis == "region" else lax.axis_index(axis) % near
        index = index + jnp.where((other ^ own) & step, 1 << i, 0)
    return index


def extras(observed, patch_map, starts, counts):
    regions = lax.axis_size("region")
    region, member = lax.axis_index("region"), lax.axis_index("member")
    result = []
    for shift in range(regions):
        owner = lax.rem(region + shift, regions), member
        pieces = [
            lax.dynamic_slice_in_dim(observed, start(*owner), count, axis=0)
            for start, count in zip(starts, counts)
        ]
        piece = jnp.concatenate(pieces + [patch_map[None]], axis=0)
        if shift:
            ring = [(i, (i + shift) % regions) for i in range(regions)]
            piece = lax.ppermute(piece, "region", ring)
        result.append(piece)
    return jnp.stack(result)


def spread_over_all(forecast, observed, patch_map):
    held, variables, rows, lon = forecast.shape
    regions, devices = lax.axis_size("region"), lax.axis_size("member")
    region, member = lax.axis_index("region"), lax.axis_index("member")
    total = regions * devices
    share = variables // total
    whole = share * total
    left = variables - whole
    chunks = [count for count in (share - share // 2, share // 2) if count]
    sent, starts, counts, begin = [], [], [], 0
    for count in chunks:
        sent.append(sent_rows(forecast[:, begin : begin + count * total], count))
        starts.append(lambda r, m, b=begin, c=count: b + (r * devices + m) * c)
        counts.append(count)
        begin += count * total
    shifts = []
    if left:
        near = devices // left
        plane = member // near
        starts.append(lambda r, m, b=begin: b + m // near)
        counts.append(1)
        for t in range(left):
            first = begin + lax.rem(plane + t, left)
            x = lax.dynamic_slice_in_dim(forecast, first, 1, axis=1).reshape(held * rows, lon)
            shifts.append(shifted(x, t * near) if t else x)
    extra = extras(observed, patch_map, starts, counts)
    hots = patch_hots(extra)
    if len(chunks) > 1:
        sent[1:], extra, hots, shifts = lax.optimization_barrier((sent[1:], extra, hots, shifts))
    order = jnp.arange(total, dtype=jnp.int32)
    results = [
        whole_fields(exchange(part), order, extra, hots, sum(chunks[:i])) for i, part in enumerate(sent)
    ]
    if left:
        field, results = plane_gather(jnp.stack(shifts), near, results)
        members = order % devices
        places = plane_index(order // devices, members, near) * left
        places = places + (plane - members // near) % left
        result = whole_fields(field[:, None], places, extra, hots, share)
        result = result[0, 0]
        shifts = [shifted(result[t], -t * near) if t else result[t] for t in range(left)]
        shifts = jnp.stack(shifts + shifts).reshape(2 * left, held, rows, lon)
        last = lax.dynamic_slice_in_dim(shifts, lax.rem(left - plane, left), left, axis=0)
        last = jnp.swapaxes(last, 0, 1)
        if len(chunks) > 1:
            results[1], last = lax.optimization_barrier((results[1], last))
    backs = []
    for result in results:
        if backs:
            result, backs[-1] = lax.optimization_barrier((result, backs[-1]))
        backs.append(exchange(result))
    parts = [kept_rows(back, rows) for back in backs]
    if left:
        parts.insert(1, last)
    out = jnp.concatenate(
        parts[:1] + [jnp.zeros((held, variables - parts[0].shape[1], rows, lon), F32)], axis=1
    )
    places = [parts[0].shape[1]] * 2
    if left:
        places = [whole, parts[0].shape[1]]
    for part, first in zip(parts[1:], places):
        out = lax.dynamic_update_slice_in_dim(out, part, first, axis=1)
    return out


def on_device(predicted_states, observed_analysis, tile_location_sequence):
    _, variables, rows, lon = predicted_states.shape
    regions, devices = lax.axis_size("region"), lax.axis_size("member")
    patch_map = patch_of_cell(tile_location_sequence[0], rows, lon)
    left = variables % (regions * devices)
    planes = left == 0 or (
        devices % left == 0 and is_power(regions) and is_power(devices // left)
    )
    if variables >= regions * devices and planes:
        return spread_over_all(predicted_states, observed_analysis, patch_map)
    smooth = smoothed_rows(predicted_states)
    everyone = lax.all_gather(smooth, "member")
    return smoothed_rows(own_members(everyone, smooth, observed_analysis, patch_map))


def solution(mesh):
    in_specs = (P("member", None, "region", None), P(None, "region", None), P("region", None))
    out_specs = P("member", None, "region", None)
    return jax.shard_map(
        on_device, mesh=mesh, in_specs=in_specs, out_specs=out_specs, check_vma=False
    )
```

```python
import functools

import jax
import jax.numpy as jnp
import numpy as np
from jax import lax
from jax.experimental import pallas as pl
from jax.experimental.pallas import tpu as pltpu
from jax.sharding import PartitionSpec as P

HALF = 32
PATCH = 128
EPS = 1e-06
STEP = 32
BLOCK = 8
VMEM = 56 * 1024 * 1024
WHOLE = 8 * 1024 * 1024
F32 = jnp.float32
BF16 = jnp.bfloat16


def bell(out_cells, in_cells):
    sigma = HALF / 2.0
    steps = np.arange(-HALF, HALF + 1)
    norm = np.sum(np.exp(-(steps**2) / (2.0 * sigma**2)))
    offset = np.asarray(in_cells)[None, :] - np.asarray(out_cells)[:, None]
    value = 0.5 * np.exp(-(offset**2) / (2.0 * sigma**2)) / norm
    value = jnp.asarray(np.where(np.abs(offset) <= HALF, value, 0.0), F32)
    return halves(value)


def halves(x):
    head = x.astype(BF16)
    return head, (x - head.astype(F32)).astype(BF16)


def lon_weights(lon):
    head, tail = bell(range(lon), range(lon))
    return jnp.block([[head, tail], [head, jnp.zeros_like(tail)]])


def lat_weights(rows, pad):
    head, tail = bell(range(rows), range(-pad, rows + pad))
    return jnp.block([[head, head], [tail, jnp.zeros_like(tail)]])


def along_lon(x, weights):
    lon = x.shape[1]
    both = jnp.concatenate(halves(x), axis=1)
    result = jnp.dot(both, weights, preferred_element_type=F32)
    return 0.5 * x + result[:, :lon] + result[:, lon:]


def along_lat(x, weights, own):
    rows = own.shape[0]
    both = jnp.concatenate(halves(x), axis=0)
    result = jnp.dot(weights, both, preferred_element_type=F32)
    return 0.5 * own + result[:rows] + result[rows:]


def patch_sums(squares, hot):
    return lax.dot_general(
        squares,
        hot,
        (((1,), (1,)), ((), ())),
        preferred_element_type=F32,
    )


def on_cells(weights, hot):
    return jnp.dot(weights, jnp.concatenate([hot, hot], axis=0), preferred_element_type=F32)


def head_and_tail(weights):
    return jnp.concatenate(halves(weights), axis=1)


def member_gaps(blocks):
    gaps = [x - pltpu.roll(x, s, 0) for x in blocks for s in range(1, BLOCK // 2 + 1)]
    for b, x in enumerate(blocks):
        for y in blocks[b + 1 :]:
            gaps.append(x - y)
            gaps += [x - pltpu.roll(y, s, 0) for s in range(1, BLOCK)]
    return gaps


def member_pulls(pulls, count):
    pulls = iter(pulls)
    sums = [0.0] * count
    for b in range(count):
        for s in range(1, BLOCK // 2 + 1):
            pull = next(pulls)
            sums[b] = sums[b] + pull
            if 2 * s != BLOCK:
                sums[b] = sums[b] - pltpu.roll(pull, BLOCK - s, 0)
    for b in range(count):
        for c in range(b + 1, count):
            for s in range(BLOCK):
                pull = next(pulls)
                sums[b] = sums[b] + pull
                sums[c] = sums[c] - (pltpu.roll(pull, BLOCK - s, 0) if s else pull)
    return sums


def field_kernel(
    regions, places_ref, field_ref, truth_ref, hots, lon_ref, lat_ref, out_ref, cells
):
    outer, _, inner, _, lon = field_ref.shape
    rows = truth_ref.shape[2]
    held = field_ref.shape[3] // rows
    devices = outer * inner // regions
    members = devices * held
    blocks = members // BLOCK
    pairs = blocks * (BLOCK // 2) + blocks * (blocks - 1) // 2 * BLOCK
    height = (pairs + blocks) * BLOCK
    steps = rows // STEP
    patches = hots.shape[1]
    scale = float(np.sqrt(PATCH))
    own = 0 if field_ref.shape[1] == 1 else pl.program_id(0)

    def shift_of(region):
        return lax.rem(places_ref[0] - region + regions, regions)

    def place(region, device, variable):
        index = places_ref[1 + region * devices + device]
        return (index, variable, 0) if inner == 1 else (index // inner, variable, index % inner)

    def smoothed(pair):
        wide = jnp.concatenate([along_lon(x, lon_ref[...]) for x in pair], axis=1)
        return along_lat(wide, lat_ref[...], wide)

    every = regions * rows
    for device in range(devices):
        pair = [
            jnp.concatenate(
                [
                    field_ref[*place(region, device, own), k * rows : (k + 1) * rows, :]
                    for region in range(regions)
                ],
                axis=0,
            )
            for k in range(held)
        ]
        result = smoothed(pair)
        for k in range(held):
            cells[pl.ds(device * held + k, every, stride=members), :] = result[
                :, k * lon : (k + 1) * lon
            ]

    for region in range(regions):
        shift = shift_of(region)

        def load(row):
            start = pl.multiple_of((region * rows + row) * members, members)
            a = [cells[pl.ds(start + b * BLOCK, BLOCK), :] for b in range(blocks)]
            truth = truth_ref[shift, 0, pl.ds(row, 1), :]
            return start, member_gaps(a) + [x - truth for x in a]

        def first(step, total):
            heads, tails = [], []
            for j in range(STEP):
                head, tail = halves(
                    jnp.concatenate([gap * gap for gap in load(step * STEP + j)[1]], axis=0)
                )
                heads.append(head)
                tails.append(tail)
            squares = jnp.concatenate(
                [jnp.concatenate(heads, axis=1), jnp.concatenate(tails, axis=1)], axis=0
            )
            return total + patch_sums(squares, hots[region * steps + step])

        total = lax.fori_loop(0, steps, first, jnp.zeros((2 * height, patches), F32))
        weights = lax.rsqrt(total[:height] + total[height:] + EPS)
        factor = jnp.where(
            lax.broadcasted_iota(jnp.int32, (height, patches), 0) < pairs * BLOCK,
            -scale / members,
            scale,
        )
        weights = head_and_tail(weights * factor)

        def second(step, carry):
            spread = on_cells(weights, hots[region * steps + step])
            for j in range(STEP):
                start, gaps = load(step * STEP + j)
                w = spread[:, j * lon : (j + 1) * lon]
                terms = [w[i * BLOCK : (i + 1) * BLOCK] * gap for i, gap in enumerate(gaps)]
                sums = member_pulls(terms[:pairs], blocks)
                for b in range(blocks):
                    cells[pl.ds(start + b * BLOCK, BLOCK), :] = sums[b] + terms[pairs + b]
            return carry

        lax.fori_loop(0, steps, second, 0)

    for device in range(devices):
        result = smoothed(
            [cells[pl.ds(device * held + k, every, stride=members), :] for k in range(held)]
        )
        for region in range(regions):
            for k in range(held):
                out_ref[*place(region, device, 0), k * rows : (k + 1) * rows, :] = result[
                    region * rows : (region + 1) * rows, k * lon : (k + 1) * lon
                ]


def hots_kernel(region_ref, extra_ref, hots):
    regions, _, rows, lon = extra_ref.shape
    _, patches, _ = hots.shape
    steps = rows // STEP
    patch = lax.broadcasted_iota(jnp.int32, (patches, lon), 0).astype(F32)
    for region in range(regions):
        shift = lax.rem(region_ref[0] - region + regions, regions)
        for row in range(rows):
            block, j = region * steps + row // STEP, row % STEP
            own = extra_ref[shift, 0, row : row + 1, :]
            hots[block, :, j * lon : (j + 1) * lon] = (patch == own).astype(BF16)


def patch_hots(extra):
    regions, variables, rows, lon = extra.shape
    shape = (regions * rows // STEP, rows * lon // PATCH, STEP * lon)
    return pl.pallas_call(
        hots_kernel,
        out_shape=jax.ShapeDtypeStruct(shape, BF16),
        grid=(1,),
        in_specs=[
            pl.BlockSpec(memory_space=pltpu.SMEM),
            pl.BlockSpec((regions, 1, rows, lon), lambda i: (0, variables - 1, 0, 0)),
        ],
        out_specs=pl.BlockSpec(shape, lambda i: (0, 0, 0)),
        compiler_params=pltpu.CompilerParams(vmem_limit_bytes=VMEM),
        name="patch_hots",
    )(lax.axis_index("region").reshape(1), extra)


def whole_fields(fields, places, extra, hots, offset):
    outer, count, inner, height, lon = fields.shape
    regions, variables, rows, _ = extra.shape
    members = outer * inner // regions * (height // rows)
    patches = rows * lon // PATCH
    every = regions * rows
    table = jnp.concatenate([lax.axis_index("region").reshape(1), places])
    block = pl.BlockSpec((outer, 1, inner, height, lon), lambda v, table: (0, v, 0, 0, 0))
    pairs = every * lon * members * (members // 2 + 1)
    return pl.pallas_call(
        functools.partial(field_kernel, regions),
        out_shape=jax.ShapeDtypeStruct(fields.shape, F32),
        grid_spec=pltpu.PrefetchScalarGridSpec(
            num_scalar_prefetch=1,
            grid=(count,),
            in_specs=[
                pl.BlockSpec(memory_space=pltpu.VMEM) if 4 * fields.size <= WHOLE else block,
                pl.BlockSpec((regions, 1, rows, lon), lambda v, table: (0, v + offset, 0, 0)),
                pl.BlockSpec(hots.shape, lambda v, table: (0, 0, 0)),
                pl.BlockSpec((2 * lon, 2 * lon), lambda v, table: (0, 0)),
                pl.BlockSpec((2 * every, 2 * every), lambda v, table: (0, 0)),
            ],
            out_specs=block,
            scratch_shapes=[
                pltpu.VMEM((every * members, lon), F32),
            ],
        ),
        compiler_params=pltpu.CompilerParams(vmem_limit_bytes=VMEM),
        cost_estimate=pl.CostEstimate(
            flops=count * pairs * patches * 8, bytes_accessed=8 * fields.size, transcendentals=0
        ),
        name="whole_fields",
    )(table, fields, extra, hots, lon_weights(lon), lat_weights(every, 0))


def smooth_kernel(own_ref, low_ref, high_ref, lon_ref, lat_ref, out_ref):
    held = own_ref.shape[0]
    for k in range(held):
        rows = [ref[k, 0] for ref in (low_ref, own_ref, high_ref)]
        wide = along_lon(jnp.concatenate(rows, axis=0), lon_ref[...])
        pad = rows[0].shape[0]
        out_ref[k, 0] = along_lat(wide, lat_ref[...], wide[pad : pad + rows[1].shape[0]])


def smoothed_rows(own):
    held, count, rows, lon = own.shape
    regions = lax.axis_size("region")
    up = [(i, i + 1) for i in range(regions - 1)]
    low = lax.ppermute(own[:, :, rows - HALF :], "region", up)
    high = lax.ppermute(own[:, :, :HALF], "region", [(b, a) for a, b in up])
    edge = pl.BlockSpec((held, 1, HALF, lon), lambda v: (0, v, 0, 0))
    block = pl.BlockSpec((held, 1, rows, lon), lambda v: (0, v, 0, 0))
    span = rows + 2 * HALF
    return pl.pallas_call(
        smooth_kernel,
        out_shape=jax.ShapeDtypeStruct(own.shape, F32),
        grid=(count,),
        in_specs=[
            block,
            edge,
            edge,
            pl.BlockSpec((2 * lon, 2 * lon), lambda v: (0, 0)),
            pl.BlockSpec((2 * rows, 2 * span), lambda v: (0, 0)),
        ],
        out_specs=block,
        compiler_params=pltpu.CompilerParams(vmem_limit_bytes=VMEM),
        name="smoothed_rows",
    )(own, low, high, lon_weights(lon), lat_weights(rows, HALF))


def share_kernel(all_ref, own_ref, truth_ref, map_ref, out_ref, cells, hots):
    devices, held, _, rows, lon = all_ref.shape
    members = devices * held
    patches = hots.shape[1]
    scale = float(np.sqrt(PATCH))
    steps = rows // STEP

    @pl.when(pl.program_id(0) == 0)
    def _():
        patch = lax.broadcasted_iota(jnp.int32, (patches, lon), 0).astype(F32)
        for row in range(rows):
            hots[row // STEP, :, row % STEP * lon : (row % STEP + 1) * lon] = (
                patch == map_ref[row : row + 1, :]
            ).astype(BF16)

    for device in range(devices):
        for k in range(held):
            cells[pl.ds(device * held + k, rows, stride=members), :] = all_ref[device, k, 0]

    def gaps(step, j):
        row = step * STEP + j
        a = cells[pl.ds(pl.multiple_of(row * members, members), members), :]
        truth = truth_ref[0, pl.ds(row, 1), :]
        result = []
        for k in range(held):
            own = own_ref[k, 0, pl.ds(row, 1), :]
            result += [own - a, jnp.broadcast_to(own - truth, (8, lon))]
        return row, result

    def first(step, total):
        columns = [
            jnp.concatenate([gap * gap for gap in gaps(step, j)[1]], axis=0) for j in range(STEP)
        ]
        squares = jnp.concatenate(halves(jnp.concatenate(columns, axis=1)), axis=0)
        return total + patch_sums(squares, hots[step])

    height = held * (members + 8)
    total = lax.fori_loop(0, steps, first, jnp.zeros((2 * height, patches), F32))
    weights = lax.rsqrt(total[:height] + total[height:] + EPS)
    place = lax.rem(lax.broadcasted_iota(jnp.int32, (height, patches), 0), members + 8)
    weights = head_and_tail(weights * jnp.where(place < members, -scale / members, scale))

    def second(step, carry):
        spread = on_cells(weights, hots[step])
        for j in range(STEP):
            row, parts = gaps(step, j)
            w = spread[:, j * lon : (j + 1) * lon]
            for k in range(held):
                base = k * (members + 8)
                pull = w[base : base + members] * parts[2 * k]
                toward = w[base + members : base + members + 1] * parts[2 * k + 1][:1]
                out_ref[k, 0, pl.ds(row, 1), :] = toward + jnp.sum(pull, axis=0, keepdims=True)
        return carry

    lax.fori_loop(0, steps, second, 0)


def own_members(everyone, smooth, truth, patch_map):
    held, count, rows, lon = smooth.shape
    devices = everyone.shape[0]
    patches = rows * lon // PATCH
    block = pl.BlockSpec((held, 1, rows, lon), lambda v: (0, v, 0, 0))
    return pl.pallas_call(
        share_kernel,
        out_shape=jax.ShapeDtypeStruct(smooth.shape, F32),
        grid=(count,),
        in_specs=[
            pl.BlockSpec((devices, held, 1, rows, lon), lambda v: (0, 0, v, 0, 0)),
            block,
            pl.BlockSpec((1, rows, lon), lambda v: (v, 0, 0)),
            pl.BlockSpec((rows, lon), lambda v: (0, 0)),
        ],
        out_specs=block,
        scratch_shapes=[
            pltpu.VMEM((rows * devices * held, lon), F32),
            pltpu.VMEM((rows // STEP, patches, STEP * lon), BF16),
        ],
        compiler_params=pltpu.CompilerParams(vmem_limit_bytes=VMEM),
        name="own_members",
    )(everyone, smooth, truth, patch_map)


def patch_of_cell(order, rows, lon):
    position = jnp.arange(rows * lon, dtype=jnp.int32)
    in_row = jnp.arange(rows, dtype=jnp.int32)[:, None] == (order // lon)[None]
    at_lon = (order % lon)[:, None] == jnp.arange(lon, dtype=jnp.int32)[None]
    patch = jnp.where(in_row, (position // PATCH)[None], 0)
    return jnp.dot(
        patch.astype(F32), at_lon.astype(F32), precision=lax.Precision.HIGHEST
    )


def exchange(blocks):
    return lax.all_to_all(blocks, ("region", "member"), 0, 0, tiled=True)


def sent_rows(x, count):
    held, variables, rows, lon = x.shape
    total = variables // count
    x = jnp.transpose(x.reshape(held, total, count, rows, lon), (1, 2, 0, 3, 4))
    return x.reshape(total, count, 1, held * rows, lon)


def kept_rows(blocks, rows):
    total, count, _, height, lon = blocks.shape
    x = blocks.reshape(total, count, height // rows, rows, lon)
    return jnp.transpose(x, (2, 0, 1, 3, 4)).reshape(height // rows, total * count, rows, lon)


def is_power(n):
    return n & (n - 1) == 0


def shifted(x, places):
    count = lax.axis_size("member")
    return lax.ppermute(x, "member", [(i, (i + places) % count) for i in range(count)])


def plane_steps(near):
    regions = lax.axis_size("region")
    far = [("region", 1 << bit) for bit in range(1, regions.bit_length() - 1)][::-1]
    beside = [("member", 1 << bit) for bit in range(near.bit_length() - 1)]
    return far + beside + [("region", 1)] * (regions > 1)


def plane_gather(x, near, beside):
    x = x[None]
    steps = plane_steps(near)
    for i, (axis, step) in enumerate(steps):
        count = lax.axis_size(axis)
        other = lax.ppermute(x, axis, [(j, j ^ step) for j in range(count)])
        if i == 0:
            other, beside = lax.optimization_barrier((other, beside))
        x = jnp.concatenate([x, other], axis=0)
    return x, beside


def plane_index(region, member, near):
    steps, index = plane_steps(near), 0
    for i, (axis, step) in enumerate(steps):
        other = region if axis == "region" else member % near
        own = lax.axis_index(axis) if axis == "region" else lax.axis_index(axis) % near
        index = index + jnp.where((other ^ own) & step, 1 << i, 0)
    return index


def extras(observed, patch_map, starts, counts):
    regions = lax.axis_size("region")
    region, member = lax.axis_index("region"), lax.axis_index("member")
    result = []
    for shift in range(regions):
        owner = lax.rem(region + shift, regions), member
        pieces = [
            lax.dynamic_slice_in_dim(observed, start(*owner), count, axis=0)
            for start, count in zip(starts, counts)
        ]
        piece = jnp.concatenate(pieces + [patch_map[None]], axis=0)
        if shift:
            ring = [(i, (i + shift) % regions) for i in range(regions)]
            piece = lax.ppermute(piece, "region", ring)
        result.append(piece)
    return jnp.stack(result)


def spread_over_all(forecast, observed, patch_map):
    held, variables, rows, lon = forecast.shape
    regions, devices = lax.axis_size("region"), lax.axis_size("member")
    region, member = lax.axis_index("region"), lax.axis_index("member")
    total = regions * devices
    share = variables // total
    whole = share * total
    left = variables - whole
    chunks = [count for count in (share // 2, share - share // 2) if count]
    sent, starts, counts, begin = [], [], [], 0
    for count in chunks:
        sent.append(sent_rows(forecast[:, begin : begin + count * total], count))
        starts.append(lambda r, m, b=begin, c=count: b + (r * devices + m) * c)
        counts.append(count)
        begin += count * total
    shifts = []
    if left:
        near = devices // left
        plane = member // near
        starts.append(lambda r, m, b=begin: b + m // near)
        counts.append(1)
        for t in range(left):
            first = begin + lax.rem(plane + t, left)
            x = lax.dynamic_slice_in_dim(forecast, first, 1, axis=1).reshape(held * rows, lon)
            shifts.append(shifted(x, t * near) if t else x)
    extra = extras(observed, patch_map, starts, counts)
    hots = patch_hots(extra)
    if len(chunks) > 1:
        sent[1:], extra, hots, shifts = lax.optimization_barrier((sent[1:], extra, hots, shifts))
    order = jnp.arange(total, dtype=jnp.int32)
    results = [
        whole_fields(exchange(part), order, extra, hots, sum(chunks[:i])) for i, part in enumerate(sent)
    ]
    if left:
        field, results[0] = plane_gather(jnp.stack(shifts), near, results[0])
        members = order % devices
        places = plane_index(order // devices, members, near) * left
        places = places + (plane - members // near) % left
        result = whole_fields(field[:, None], places, extra, hots, share)
        result = result[0, 0]
        results[0], result = lax.optimization_barrier((results[0], result))
        shifts = [shifted(result[t], -t * near) if t else result[t] for t in range(left)]
        if len(chunks) > 1:
            shifts, results[1] = lax.optimization_barrier((shifts, results[1]))
        shifts = jnp.stack(shifts + shifts).reshape(2 * left, held, rows, lon)
        last = lax.dynamic_slice_in_dim(shifts, lax.rem(left - plane, left), left, axis=0)
        last = jnp.swapaxes(last, 0, 1)
    backs = []
    for result in results:
        if backs:
            result, backs[-1] = lax.optimization_barrier((result, backs[-1]))
        backs.append(exchange(result))
    parts = [kept_rows(back, rows) for back in backs]
    if left:
        parts.insert(1, last)
    out = jnp.concatenate(
        parts[:1] + [jnp.zeros((held, variables - parts[0].shape[1], rows, lon), F32)], axis=1
    )
    places = [parts[0].shape[1]] * 2
    if left:
        places = [whole, parts[0].shape[1]]
    for part, first in zip(parts[1:], places):
        out = lax.dynamic_update_slice_in_dim(out, part, first, axis=1)
    return out


def on_device(predicted_states, observed_analysis, tile_location_sequence):
    _, variables, rows, lon = predicted_states.shape
    regions, devices = lax.axis_size("region"), lax.axis_size("member")
    patch_map = patch_of_cell(tile_location_sequence[0], rows, lon)
    left = variables % (regions * devices)
    planes = left == 0 or (
        devices % left == 0 and is_power(regions) and is_power(devices // left)
    )
    if variables >= regions * devices and planes:
        return spread_over_all(predicted_states, observed_analysis, patch_map)
    smooth = smoothed_rows(predicted_states)
    everyone = lax.all_gather(smooth, "member")
    return smoothed_rows(own_members(everyone, smooth, observed_analysis, patch_map))


def solution(mesh):
    in_specs = (P("member", None, "region", None), P(None, "region", None), P("region", None))
    out_specs = P("member", None, "region", None)
    return jax.shard_map(
        on_device, mesh=mesh, in_specs=in_specs, out_specs=out_specs, check_vma=False
    )
```
